32 devices in a mesh: px: 4 (over x, core), py: 8 (over z, y).
Axes of the slice: x: 2, y: 2, z: 4, core: 2. Of those that a mesh axis runs over, the one named last changes fastest.
Arguments:
- theta_field: float32 [32, 64, 1024], P(None, 'px', 'py'), may hold values from -6 to 6
- wind_u: float32 [32, 64, 1024], P(None, 'px', 'py'), may hold values from -6 to 6
- wind_v: float32 [32, 64, 1024], P(None, 'px', 'py'), may hold values from -6 to 6
- hyper_coef: float32 [32], replicated, may hold values from 0.002 to 0.02
- damp_coef: float32 [32], replicated, may hold values from 0.05 to 0.4
- obs_cells: int32 [32, 32, 512], P(('px', 'py')), may hold values from 0 to 1918, as said below
- obs_levels: int32 [32, 32, 512], P(('px', 'py')), may hold values from 0 to 30
- obs_bary: float32 [32, 32, 3, 512], P(('px', 'py')), may hold values from 0 to 1, as said below
- obs_vfrac: float32 [32, 32, 512], P(('px', 'py')), may hold values from 0 to 1
- obs_values: float32 [32, 32, 512], P(('px', 'py')), may hold values from -6 to 6
- obs_mask: int32 [32, 32, 512], P(('px', 'py')), may hold values from 0 to 1, as said below
Outputs:
- theta_next: float32 [32, 64, 1024], P(None, 'px', 'py')
- wind_u_next: float32 [32, 64, 1024], P(None, 'px', 'py')
- wind_v_next: float32 [32, 64, 1024], P(None, 'px', 'py')
- departures: float32 [32, 32, 512], P(('px', 'py'))
The draws below stay inside these ranges and needn't reach their ends.
Inputs may be any that keep to these rules, and one draw needn't show every extreme that they name: obs_cells is r * 128 + c with r below 15 and c below 127. `obs_bary`: each row of three weights is positive and sums to one. `obs_mask`: in every draw some destination patch has all 512 slots used from every owner.
All inputs are finite; a program needn't handle non-finite values.
Results may differ from the reference program's by a relative error of at most 0.000084.
Values sent between devices are 32-bit elements; how exact they have to be, the bound alone decides.
A program may use at most 64 MiB of HBM per device.

```python
import math
import jax
import jax.numpy as jnp

LEV = 32
CX = 16
CY = 128
PATCHES = 32
SLOT = 512
NX = 64
NY = 1024
N_PY = 8


def draw_obs_cells(key, part):
    key_row, key_col = jax.random.split(jax.random.fold_in(key, 11))
    shape = (PATCHES, PATCHES, SLOT)
    rows = jax.random.randint(key_row, shape, 0, CX - 1)
    cols = jax.random.randint(key_col, shape, 0, CY - 1)
    return (rows * CY + cols).astype(jnp.int32)


def draw_obs_bary(key, part):
    raw = jax.random.uniform(jax.random.fold_in(key, 12), (PATCHES, PATCHES, 3, SLOT), jnp.float32, 0.05, 1.0)
    return raw / jnp.sum(raw, axis=2, keepdims=True)


def draw_obs_mask(key, part):
    key_level, key_full, key_slot = jax.random.split(jax.random.fold_in(key, 13), 3)
    levels = jax.random.randint(key_level, (PATCHES,), 250, 1001)
    full_one = jax.random.randint(key_full, (), 0, PATCHES)
    levels = jnp.where(jnp.arange(PATCHES) == full_one, 1000, levels)
    slots = jax.random.randint(key_slot, (PATCHES, PATCHES, SLOT), 0, 1000)
    return (slots < levels[None, :, None]).astype(jnp.int32)


def with_ends(values, key, smallest, top_value):
    index_at = [jax.random.randint(jax.random.fold_in(key, axis), (), 0, length) for axis, length in enumerate(values.shape)]
    longest = values.shape.index(max(values.shape))
    next_to = index_at[:longest] + [(index_at[longest] + 1) % values.shape[longest]] + index_at[longest + 1:]
    return values.at[tuple(index_at)].set(smallest).at[tuple(next_to)].set(top_value)


def level_of(stream_key, shape, cuts, smallest, high):
    gain, own = 1.0, jax.random.fold_in(stream_key, 6)
    for axis_at, blocks in cuts:
        steps = jnp.exp(jax.random.uniform(jax.random.fold_in(own, axis_at), (blocks,), jnp.float32, smallest / len(cuts), high / len(cuts)))
        gain = gain * jnp.repeat(steps, shape[axis_at] // blocks).reshape([-1 if axis == axis_at else 1 for axis in range(len(shape))])
    return gain


def gaussian(stream_key, dims, scale, most, pieces=(), held_as=jnp.bfloat16):
    values = scale * jax.random.normal(stream_key, dims, jnp.float32)
    if pieces:
        values = values * level_of(stream_key, dims, pieces, -0.22, 0.18)
    return jnp.clip(values, -most, most).astype(held_as)


def setup_inputs(seed: int = 0) -> dict:
    keys = jax.random.split(jax.random.key(seed), 12)
    theta_field = gaussian(keys[0], (LEV, NX, NY), 1.0, 6.0, ((1, 4), (2, 8)), jnp.float32)
    wind_u = gaussian(keys[1], (LEV, NX, NY), 1.0, 6.0, ((1, 4), (2, 8)), jnp.float32)
    wind_v = gaussian(keys[2], (LEV, NX, NY), 1.0, 6.0, ((1, 4), (2, 8)), jnp.float32)
    hyper_coef = jnp.clip(jnp.exp(jax.random.uniform(keys[3], (LEV,), jnp.float32, math.log(0.002), math.log(0.02))), 0.002, 0.02)
    damp_coef = jnp.clip(jnp.exp(jax.random.uniform(keys[4], (LEV,), jnp.float32, math.log(0.05), math.log(0.4))), 0.05, 0.4)
    obs_cells = draw_obs_cells(jax.random.fold_in(keys[11], 71), 0)
    obs_levels = with_ends(jax.random.randint(keys[6], (PATCHES, PATCHES, SLOT), 0, LEV - 1), jax.random.fold_in(keys[6], 1), 0, (LEV - 1) - 1).astype(jnp.int32)
    obs_bary = draw_obs_bary(jax.random.fold_in(keys[11], 71), 0)
    obs_vfrac = jnp.clip(1.0 * jax.random.uniform(keys[8], (PATCHES, PATCHES, SLOT), jnp.float32) ** level_of(keys[8], (PATCHES, PATCHES, SLOT), ((0, 32),), -0.2, 0.2), 0.0, 1.0)
    obs_values = gaussian(keys[9], (PATCHES, PATCHES, SLOT), 1.0, 6.0, ((0, 32),), jnp.float32)
    obs_mask = draw_obs_mask(jax.random.fold_in(keys[11], 71), 0)
    return dict(theta_field=theta_field, wind_u=wind_u, wind_v=wind_v, hyper_coef=hyper_coef, damp_coef=damp_coef, obs_cells=obs_cells, obs_levels=obs_levels, obs_bary=obs_bary, obs_vfrac=obs_vfrac, obs_values=obs_values, obs_mask=obs_mask)


def roll_view(field, step_i, step_j):
    return jnp.roll(field, (-step_i, -step_j), axis=(-2, -1))


def laplace(field):
    total = roll_view(field, 1, 0) + roll_view(field, -1, 0)
    total = total + roll_view(field, 0, 1) + roll_view(field, 0, -1)
    total = total + roll_view(field, 1, -1) + roll_view(field, -1, 1)
    return total - 6.0 * field


def diff_x(field):
    return (roll_view(field, 1, 0) - roll_view(field, -1, 0)) * 0.5


def diff_y(field):
    return (roll_view(field, 0, 1) - roll_view(field, 0, -1)) * 0.5


def reference(theta_field, wind_u, wind_v, hyper_coef, damp_coef, obs_cells, obs_levels, obs_bary, obs_vfrac, obs_values, obs_mask):
    coef = hyper_coef[:, None, None]
    damp = damp_coef[:, None, None]
    divergence = diff_x(wind_u) + diff_y(wind_v)
    theta_next = theta_field - coef * laplace(laplace(theta_field)) - 0.5 * (wind_u * diff_x(theta_field) + wind_v * diff_y(theta_field))
    wind_u_next = wind_u - coef * laplace(laplace(wind_u)) + damp * diff_x(divergence)
    wind_v_next = wind_v - coef * laplace(laplace(wind_v)) + damp * diff_y(divergence)
    dest = jnp.arange(PATCHES, dtype=jnp.int32)[None, :, None]
    row_base = (dest // N_PY) * CX + obs_cells // CY
    col_base = (dest % N_PY) * CY + obs_cells % CY
    plane = NX * NY
    base = obs_levels * plane + row_base * NY + col_base
    flat = theta_next.reshape(-1)
    above = obs_vfrac
    model = jnp.zeros(obs_values.shape, jnp.float32)
    for index, offset in enumerate((0, NY, 1)):
        cell_id = (base + offset).astype(jnp.int32)
        column = (1.0 - above) * flat[cell_id] + above * flat[cell_id + plane]
        model = model + obs_bary[:, :, index, :] * column
    departures = obs_mask.astype(jnp.float32) * (obs_values - model)
    return theta_next, wind_u_next, wind_v_next, departures
```

```python
import functools

import jax
import jax.numpy as jnp
from jax import lax
from jax.experimental import pallas as pl
from jax.experimental.pallas import tpu as pltpu
from jax.sharding import PartitionSpec as P

MESH = pl.DeviceIdType.MESH
FIELDS = 5
CORNERS = ((-1, -1), (-1, 1), (1, -1), (1, 1))


def laplace(x):
    rows, cols = x.shape
    below = pltpu.roll(x, rows - 1, 0)
    above = pltpu.roll(x, 1, 0)
    return (
        below
        + above
        + pltpu.roll(x + above, cols - 1, 1)
        + pltpu.roll(x + below, 1, 1)
        - 6.0 * x
    )


def diff_x(x):
    return (pltpu.roll(x, x.shape[0] - 1, 0) - pltpu.roll(x, 1, 0)) * 0.5


def diff_y(x):
    return (pltpu.roll(x, x.shape[1] - 1, 1) - pltpu.roll(x, 1, 1)) * 0.5


def kernel(
    sizes,
    hyper,
    damp,
    u_ref,
    v_ref,
    t_ref,
    cells_ref,
    levels_ref,
    bary_ref,
    vfrac_ref,
    values_ref,
    mask_ref,
    u_out,
    v_out,
    t_out,
    dep_out,
    out_buf,
    in_buf,
    model_buf,
    model_in,
    row_buf,
    row_in,
    col_buf,
    col_in,
    corner_in,
    table,
    obs_send,
    obs_recv,
    model_send,
    model_recv,
    halo_send,
    halo_recv,
):
    n_px, n_py, tiles = sizes
    count = n_px * n_py
    levs, rows, cols = t_ref.shape
    px = lax.axis_index("px")
    py = lax.axis_index("py")
    me = px * n_py + py
    fields = (u_ref, v_ref, t_ref)

    def place(dev):
        return (dev // n_py, dev % n_py)

    barrier = pltpu.get_barrier_semaphore()

    def greet(k, _):
        pl.semaphore_signal(
            barrier, inc=1, device_id=place(lax.rem(me + k, count)), device_id_type=MESH
        )
        return 0

    lax.fori_loop(1, count, greet, 0)

    row8 = lax.broadcasted_iota(jnp.int32, (8, cols), 0)
    lane16 = lax.broadcasted_iota(jnp.int32, (rows, cols), 1)
    lane24 = lax.broadcasted_iota(jnp.int32, (rows + 8, cols), 1)

    def pack_edges(g, _):
        edge = jnp.zeros((rows, cols), jnp.float32)
        for f, ref in enumerate(fields):
            for half in range(2):
                top = jnp.zeros((8, cols), jnp.float32)
                bottom = top
                for i in range(4):
                    at = half * 4 + i
                    x = ref[g * 8 + at]
                    base = 16 * at + 4 * f
                    edge = jnp.where(
                        lane16 // 4 == base // 4, pltpu.roll(x, (base + 2) % cols, 1), edge
                    )
                    here = row8 // 2 == i
                    head = x[:8]
                    tail = x[rows - 8 :]
                    if i:
                        head = pltpu.roll(head, 2 * i, 0)
                    if (2 * i + 2) % 8:
                        tail = pltpu.roll(tail, 2 * i + 2, 0)
                    top = jnp.where(here, head, top)
                    bottom = jnp.where(here, tail, bottom)
                row_buf[0, f, g * 2 + half] = top
                row_buf[1, f, g * 2 + half] = bottom
        col_buf[g] = edge
        return 0

    lax.fori_loop(0, levs // 8, pack_edges, 0)

    def pack_obs(g, _):
        lines = pl.ds(pl.multiple_of(g * 8, 8), 8)
        for t in range(tiles):
            part = pl.ds(t * 128, 128)
            whole = (
                cells_ref[0, lines, part].astype(jnp.float32),
                levels_ref[0, lines, part].astype(jnp.float32),
                vfrac_ref[0, lines, part],
            )
            for i in range(8):
                for f, x in enumerate(whole):
                    out_buf[g * 8 + i, f, pl.ds(t, 1)] = x[i : i + 1]
                for j in range(2):
                    out_buf[g * 8 + i, 3 + j, pl.ds(t, 1)] = bary_ref[0, g * 8 + i, pl.ds(j, 1), part]
        return 0

    lax.fori_loop(0, count // 8, pack_obs, 0)
    in_buf[me] = out_buf[me]

    pl.semaphore_wait(barrier, count - 1)

    def remote(src, dst, send, recv, dev):
        return pltpu.make_async_remote_copy(
            src_ref=src,
            dst_ref=dst,
            send_sem=send,
            recv_sem=recv,
            device_id=dev,
            device_id_type=MESH,
        )

    up = lax.rem(px + n_px - 1, n_px)
    down = lax.rem(px + 1, n_px)
    left = lax.rem(py + n_py - 1, n_py)
    right = lax.rem(py + 1, n_py)
    halo = []

    def edge_copy(src, dst, dev):
        k = len(halo)
        halo.append(remote(src, dst, halo_send.at[k], halo_recv.at[k], dev))

    edge_copy(row_buf.at[0], row_in.at[0], (up, py))
    edge_copy(row_buf.at[1], row_in.at[1], (down, py))
    edge_copy(col_buf, col_in.at[0], (px, left))
    edge_copy(col_buf, col_in.at[1], (px, right))
    for k, (step_x, step_y) in enumerate(CORNERS):
        part = pl.ds(0, 8) if step_x < 0 else pl.ds(rows - 8, 8)
        edge_copy(
            col_buf.at[:, part],
            corner_in.at[k],
            (up if step_x < 0 else down, left if step_y < 0 else right),
        )
    for copy in halo:
        copy.start()

    def obs_copy(k):
        dev = lax.rem(me + k, count)
        return remote(
            out_buf.at[dev], in_buf.at[me], obs_send.at[dev], obs_recv.at[me], place(dev)
        )

    def send_obs(k, _):
        obs_copy(k).start()
        return 0

    lax.fori_loop(1, count, send_obs, 0)
    for copy in halo:
        copy.wait()

    def advance(g, _):
        low = row8 < 4
        from_left = jnp.concatenate(
            [col_in[1, g // 2], jnp.where(low, corner_in[1, g // 2], corner_in[3, g // 2])], axis=0
        )
        from_right = jnp.concatenate(
            [col_in[0, g // 2], jnp.where(low, corner_in[0, g // 2], corner_in[2, g // 2])], axis=0
        )
        sides = jnp.where(lane24 % 4 < 2, from_left, from_right)
        sides = pltpu.roll(sides, 64 * (g % 2), 1)
        for i in range(4):
            lev = g * 4 + i
            whole = []
            for f, ref in enumerate(fields):
                below = row_in[0, f, g]
                above = row_in[1, f, g]
                if i:
                    below = pltpu.roll(below, 8 - 2 * i, 0)
                if (6 - 2 * i) % 8:
                    above = pltpu.roll(above, 6 - 2 * i, 0)
                middle = jnp.concatenate([ref[lev], jnp.where(low, below, above)], axis=0)
                base = 16 * i + 4 * f
                edge = pltpu.roll(sides, (2 * cols - base - 2) % cols, 1)
                whole.append(jnp.concatenate([middle, edge], axis=1))
            u, v, t = whole
            coef = hyper[lev]
            rate = damp[lev]
            div = diff_x(u) + diff_y(v)
            u_in = u[:rows, :cols]
            v_in = v[:rows, :cols]
            t_in = t[:rows, :cols]
            u_out[lev] = (
                u_in
                - coef * laplace(laplace(u))[:rows, :cols]
                + rate * diff_x(div)[:rows, :cols]
            )
            v_out[lev] = (
                v_in
                - coef * laplace(laplace(v))[:rows, :cols]
                + rate * diff_y(div)[:rows, :cols]
            )
            drift = u_in * diff_x(t)[:rows, :cols] + v_in * diff_y(t)[:rows, :cols]
            t_out[lev] = t_in - coef * laplace(laplace(t))[:rows, :cols] - 0.5 * drift
        return 0

    lax.fori_loop(0, levs // 4, advance, 0)

    for r in range(rows):
        line = t_out[:, r, :]
        for step in range(2):
            if step:
                line = pltpu.roll(line, cols - 1, 1)
            high = line.astype(jnp.bfloat16)
            low = (line - high.astype(jnp.float32)).astype(jnp.bfloat16)
            at = (r * 2 + step) * levs
            table[pl.ds(at, levs), pl.ds(0, cols)] = high
            table[pl.ds(at, levs), pl.ds(cols, cols)] = low

    group = 2 if tiles % 2 == 0 else 1
    width = group * 128
    col_iota = lax.broadcasted_iota(jnp.int32, (cols, width), 0)
    lev_iota = lax.broadcasted_iota(jnp.int32, (levs, width), 0)

    def interpolate(k, _):
        src = lax.rem(me + count - k, count)

        @pl.when(k > 0)
        def _():
            remote(
                out_buf.at[src], in_buf.at[src], obs_send.at[src], obs_recv.at[src], place(src)
            ).wait_recv()

        for part in range(tiles // group):

            def piece(f):
                return jnp.concatenate(
                    [in_buf[src, f, pl.ds(part * group + t, 1)] for t in range(group)], axis=1
                )

            cell = piece(0).astype(jnp.int32)
            level = piece(1).astype(jnp.int32)
            frac = piece(2)
            w0 = piece(3)
            w1 = piece(4)
            w2 = 1.0 - w0 - w1
            col = cell & (cols - 1)
            row = cell // cols
            hot = jnp.where(col_iota == col, 1.0, 0.0).astype(jnp.bfloat16)
            hot = jnp.concatenate([hot, hot], axis=0)
            found = jnp.dot(table[...], hot, preferred_element_type=jnp.float32)
            zero = jnp.zeros((levs, width), jnp.float32)
            base, nxt, side = zero, zero, zero
            before = None
            for r in range(rows):
                at = r * 2 * levs
                line = found[at : at + levs]
                if before is not None:
                    nxt = jnp.where(before, line, nxt)
                if r < rows - 1:
                    here = jnp.broadcast_to(row == r, (levs, width))
                    base = jnp.where(here, line, base)
                    side = jnp.where(here, found[at + levs : at + 2 * levs], side)
                    before = here
            column = w0 * base + w1 * nxt + w2 * side
            share = jnp.where(lev_iota == level, 1.0 - frac, 0.0)
            share = jnp.where(lev_iota == level + 1, frac, share)
            model = jnp.sum(column * share, axis=0, keepdims=True)
            for t in range(group):
                model_buf[src, pl.ds(part * group + t, 1)] = model[:, t * 128 : (t + 1) * 128]

        @pl.when(k > 0)
        def _():
            remote(
                model_buf.at[src],
                model_in.at[me],
                model_send.at[src],
                model_recv.at[me],
                place(src),
            ).start()

        return 0

    lax.fori_loop(0, count, interpolate, 0)
    model_in[me] = model_buf[me]

    def finish(k, _):
        dev = lax.rem(me + count - k, count)

        obs_copy(k).wait_send()
        remote(
            model_buf.at[dev],
            model_in.at[dev],
            model_send.at[dev],
            model_recv.at[dev],
            place(dev),
        ).wait()
        return 0

    lax.fori_loop(1, count, finish, 0)

    def depart(g, _):
        lines = pl.ds(pl.multiple_of(g * 8, 8), 8)
        for t in range(tiles):
            part = pl.ds(t * 128, 128)
            model = jnp.concatenate(
                [model_in[g * 8 + i, pl.ds(t, 1)] for i in range(8)], axis=0
            )
            dep_out[0, lines, part] = mask_ref[0, lines, part].astype(jnp.float32) * (
                values_ref[0, lines, part] - model
            )
        return 0

    lax.fori_loop(0, count // 8, depart, 0)


def solution(mesh):
    n_px = mesh.shape["px"]
    n_py = mesh.shape["py"]
    count = n_px * n_py

    def on_device(
        theta_field,
        wind_u,
        wind_v,
        hyper_coef,
        damp_coef,
        obs_cells,
        obs_levels,
        obs_bary,
        obs_vfrac,
        obs_values,
        obs_mask,
    ):
        levs, rows, cols = theta_field.shape
        tiles = obs_values.shape[2] // 128
        vmem = pl.BlockSpec(memory_space=pltpu.VMEM)
        smem = pl.BlockSpec(memory_space=pltpu.SMEM)
        f32 = jnp.float32
        field = jax.ShapeDtypeStruct(theta_field.shape, f32)
        u_next, v_next, t_next, dep = pl.pallas_call(
            functools.partial(kernel, (n_px, n_py, tiles)),
            out_shape=(field, field, field, jax.ShapeDtypeStruct(obs_values.shape, f32)),
            in_specs=[smem] * 2 + [vmem] * 9,
            out_specs=[vmem] * 4,
            scratch_shapes=[
                pltpu.VMEM((count, FIELDS, tiles, 128), f32),
                pltpu.VMEM((count, FIELDS, tiles, 128), f32),
                pltpu.VMEM((count, tiles, 128), f32),
                pltpu.VMEM((count, tiles, 128), f32),
                pltpu.VMEM((2, 3, levs // 4, 8, cols), f32),
                pltpu.VMEM((2, 3, levs // 4, 8, cols), f32),
                pltpu.VMEM((levs // 8, rows, cols), f32),
                pltpu.VMEM((2, levs // 8, rows, cols), f32),
                pltpu.VMEM((4, levs // 8, 8, cols), f32),
                pltpu.VMEM((rows * 2 * levs, 2 * cols), jnp.bfloat16),
                pltpu.SemaphoreType.DMA((count,)),
                pltpu.SemaphoreType.DMA((count,)),
                pltpu.SemaphoreType.DMA((count,)),
                pltpu.SemaphoreType.DMA((count,)),
                pltpu.SemaphoreType.DMA((8,)),
                pltpu.SemaphoreType.DMA((8,)),
            ],
            compiler_params=pltpu.CompilerParams(
                collective_id=0, has_side_effects=True, vmem_limit_bytes=40 * 1024 * 1024
            ),
        )(
            hyper_coef,
            damp_coef,
            wind_u,
            wind_v,
            theta_field,
            obs_cells,
            obs_levels,
            obs_bary,
            obs_vfrac,
            obs_values,
            obs_mask,
        )
        return (t_next, u_next, v_next, dep)

    cells = P(None, "px", "py")
    obs = P(("px", "py"), None, None)
    return jax.shard_map(
        on_device,
        mesh=mesh,
        in_specs=(cells, cells, cells, P(), P(), obs, obs, P(("px", "py"), None, None, None), obs, obs, obs),
        out_specs=(cells, cells, cells, obs),
        check_vma=False,
    )
```

```python
import functools

import jax
import jax.numpy as jnp
from jax import lax
from jax.experimental import pallas as pl
from jax.experimental.pallas import tpu as pltpu
from jax.sharding import PartitionSpec as P

MESH = pl.DeviceIdType.MESH
FIELDS = 5
CORNERS = ((-1, -1), (-1, 1), (1, -1), (1, 1))


def laplace(x):
    rows, cols = x.shape
    below = pltpu.roll(x, rows - 1, 0)
    above = pltpu.roll(x, 1, 0)
    return (
        below
        + above
        + pltpu.roll(x + above, cols - 1, 1)
        + pltpu.roll(x + below, 1, 1)
        - 6.0 * x
    )


def diff_x(x):
    return (pltpu.roll(x, x.shape[0] - 1, 0) - pltpu.roll(x, 1, 0)) * 0.5


def diff_y(x):
    return (pltpu.roll(x, x.shape[1] - 1, 1) - pltpu.roll(x, 1, 1)) * 0.5


def kernel(
    sizes,
    hyper,
    damp,
    u_hbm,
    v_hbm,
    t_hbm,
    cells_hbm,
    levels_hbm,
    bary_hbm,
    vfrac_hbm,
    values_hbm,
    mask_hbm,
    u_res,
    v_res,
    t_res,
    dep_res,
    u_ref,
    v_ref,
    t_ref,
    cells_ref,
    levels_ref,
    bary_ref,
    vfrac_ref,
    values_ref,
    mask_ref,
    u_out,
    v_out,
    t_out,
    dep_out,
    out_buf,
    in_buf,
    model_buf,
    model_in,
    row_buf,
    row_in,
    col_buf,
    col_in,
    corner_in,
    table,
    obs_send,
    obs_recv,
    model_send,
    model_recv,
    halo_send,
    halo_recv,
    load_sem,
    store_sem,
):
    n_px, n_py, tiles = sizes
    count = n_px * n_py
    levs, rows, cols = t_ref.shape
    px = lax.axis_index("px")
    py = lax.axis_index("py")
    me = px * n_py + py
    fields = (u_ref, v_ref, t_ref)

    def place(dev):
        return (dev // n_py, dev % n_py)

    loads = [
        pltpu.make_async_copy(src, dst, load_sem.at[k])
        for k, (src, dst) in enumerate(
            (
                (u_hbm, u_ref),
                (v_hbm, v_ref),
                (t_hbm, t_ref),
                (cells_hbm, cells_ref),
                (levels_hbm, levels_ref),
                (vfrac_hbm, vfrac_ref),
                (bary_hbm, bary_ref),
                (values_hbm, values_ref),
                (mask_hbm, mask_ref),
            )
        )
    ]
    for load in loads:
        load.start()

    barrier = pltpu.get_barrier_semaphore()

    def greet(k, _):
        pl.semaphore_signal(
            barrier, inc=1, device_id=place(lax.rem(me + k, count)), device_id_type=MESH
        )
        return 0

    lax.fori_loop(1, count, greet, 0)

    row8 = lax.broadcasted_iota(jnp.int32, (8, cols), 0)
    lane16 = lax.broadcasted_iota(jnp.int32, (rows, cols), 1)
    lane24 = lax.broadcasted_iota(jnp.int32, (rows + 8, cols), 1)

    for load in loads[:3]:
        load.wait()

    def pack_edges(g, _):
        edge = jnp.zeros((rows, cols), jnp.float32)
        for f, ref in enumerate(fields):
            for half in range(2):
                top = jnp.zeros((8, cols), jnp.float32)
                bottom = top
                for i in range(4):
                    at = half * 4 + i
                    x = ref[g * 8 + at]
                    base = 16 * at + 4 * f
                    edge = jnp.where(
                        lane16 // 4 == base // 4, pltpu.roll(x, (base + 2) % cols, 1), edge
                    )
                    here = row8 // 2 == i
                    head = x[:8]
                    tail = x[rows - 8 :]
                    if i:
                        head = pltpu.roll(head, 2 * i, 0)
                    if (2 * i + 2) % 8:
                        tail = pltpu.roll(tail, 2 * i + 2, 0)
                    top = jnp.where(here, head, top)
                    bottom = jnp.where(here, tail, bottom)
                row_buf[0, f, g * 2 + half] = top
                row_buf[1, f, g * 2 + half] = bottom
        col_buf[g] = edge
        return 0

    lax.fori_loop(0, levs // 8, pack_edges, 0)

    for load in loads[3:]:
        load.wait()

    def pack_obs(g, _):
        lines = pl.ds(pl.multiple_of(g * 8, 8), 8)
        for t in range(tiles):
            part = pl.ds(t * 128, 128)
            whole = (
                cells_ref[0, lines, part].astype(jnp.float32),
                levels_ref[0, lines, part].astype(jnp.float32),
                vfrac_ref[0, lines, part],
                bary_ref[0, 0, lines, part],
                bary_ref[0, 1, lines, part],
            )
            for i in range(8):
                for f, x in enumerate(whole):
                    out_buf[g * 8 + i, f, pl.ds(t, 1)] = x[i : i + 1]
        return 0

    lax.fori_loop(0, count // 8, pack_obs, 0)
    in_buf[me] = out_buf[me]

    pl.semaphore_wait(barrier, count - 1)

    def remote(src, dst, send, recv, dev):
        return pltpu.make_async_remote_copy(
            src_ref=src,
            dst_ref=dst,
            send_sem=send,
            recv_sem=recv,
            device_id=dev,
            device_id_type=MESH,
        )

    up = lax.rem(px + n_px - 1, n_px)
    down = lax.rem(px + 1, n_px)
    left = lax.rem(py + n_py - 1, n_py)
    right = lax.rem(py + 1, n_py)
    halo = []

    def edge_copy(src, dst, dev):
        k = len(halo)
        halo.append(remote(src, dst, halo_send.at[k], halo_recv.at[k], dev))

    edge_copy(row_buf.at[0], row_in.at[0], (up, py))
    edge_copy(row_buf.at[1], row_in.at[1], (down, py))
    edge_copy(col_buf, col_in.at[0], (px, left))
    edge_copy(col_buf, col_in.at[1], (px, right))
    for k, (step_x, step_y) in enumerate(CORNERS):
        part = pl.ds(0, 8) if step_x < 0 else pl.ds(rows - 8, 8)
        edge_copy(
            col_buf.at[:, part],
            corner_in.at[k],
            (up if step_x < 0 else down, left if step_y < 0 else right),
        )
    for copy in halo:
        copy.start()

    def obs_copy(k):
        dev = lax.rem(me + k, count)
        return remote(
            out_buf.at[dev], in_buf.at[me], obs_send.at[dev], obs_recv.at[me], place(dev)
        )

    def send_obs(k, _):
        obs_copy(k).start()
        return 0

    lax.fori_loop(1, count, send_obs, 0)
    for copy in halo:
        copy.wait()

    def advance(g, _):
        low = row8 < 4
        from_left = jnp.concatenate(
            [col_in[1, g // 2], jnp.where(low, corner_in[1, g // 2], corner_in[3, g // 2])], axis=0
        )
        from_right = jnp.concatenate(
            [col_in[0, g // 2], jnp.where(low, corner_in[0, g // 2], corner_in[2, g // 2])], axis=0
        )
        sides = jnp.where(lane24 % 4 < 2, from_left, from_right)
        sides = pltpu.roll(sides, 64 * (g % 2), 1)
        for i in range(4):
            lev = g * 4 + i
            whole = []
            for f, ref in enumerate(fields):
                below = row_in[0, f, g]
                above = row_in[1, f, g]
                if i:
                    below = pltpu.roll(below, 8 - 2 * i, 0)
                if (6 - 2 * i) % 8:
                    above = pltpu.roll(above, 6 - 2 * i, 0)
                middle = jnp.concatenate([ref[lev], jnp.where(low, below, above)], axis=0)
                base = 16 * i + 4 * f
                edge = pltpu.roll(sides, (2 * cols - base - 2) % cols, 1)
                whole.append(jnp.concatenate([middle, edge], axis=1))
            u, v, t = whole
            coef = hyper[lev]
            rate = damp[lev]
            div = diff_x(u) + diff_y(v)
            u_in = u[:rows, :cols]
            v_in = v[:rows, :cols]
            t_in = t[:rows, :cols]
            u_out[lev] = (
                u_in
                - coef * laplace(laplace(u))[:rows, :cols]
                + rate * diff_x(div)[:rows, :cols]
            )
            v_out[lev] = (
                v_in
                - coef * laplace(laplace(v))[:rows, :cols]
                + rate * diff_y(div)[:rows, :cols]
            )
            drift = u_in * diff_x(t)[:rows, :cols] + v_in * diff_y(t)[:rows, :cols]
            t_out[lev] = t_in - coef * laplace(laplace(t))[:rows, :cols] - 0.5 * drift
        return 0

    lax.fori_loop(0, levs // 4, advance, 0)
    stores = [
        pltpu.make_async_copy(src, dst, store_sem.at[k])
        for k, (src, dst) in enumerate(
            ((u_out, u_res), (v_out, v_res), (t_out, t_res), (dep_out, dep_res))
        )
    ]
    for store in stores[:3]:
        store.start()

    for r in range(rows):
        line = t_out[:, r, :]
        for step in range(2):
            if step:
                line = pltpu.roll(line, cols - 1, 1)
            high = line.astype(jnp.bfloat16)
            low = (line - high.astype(jnp.float32)).astype(jnp.bfloat16)
            at = (r * 2 + step) * levs
            table[pl.ds(at, levs), pl.ds(0, cols)] = high
            table[pl.ds(at, levs), pl.ds(cols, cols)] = low

    chunks = max(1, tiles // 2)
    width = 256
    step_rows = 2 * levs
    col_iota = lax.broadcasted_iota(jnp.int32, (cols, width), 0)
    lev_iota = lax.broadcasted_iota(jnp.int32, (levs, width), 0)

    def piece(src, f, j):
        return jnp.concatenate(
            [in_buf[src, f, pl.ds(min(j * 2 + t, tiles - 1), 1)] for t in range(2)], axis=1
        )

    def stage(k):
        src = lax.rem(me + count - k, count)
        for j in range(chunks):
            col = piece(src, 0, j).astype(jnp.int32) & (cols - 1)
            hot = jnp.where(col_iota == col, 1.0, 0.0).astype(jnp.bfloat16)
            pltpu.matmul_push_rhs(jnp.concatenate([hot, hot], axis=0), 0, j)

    def run(accs):
        def feed(j, r):
            pltpu.matmul_acc_lhs(
                accs[j][r],
                table[pl.ds(r * step_rows, step_rows)],
                load_staged_rhs=0 if r == 0 else None,
            )

        def consume(k, more):
            src = lax.rem(me + count - k, count)
            for j in range(chunks):
                row = piece(src, 0, j).astype(jnp.int32) // cols
                zero = jnp.zeros((levs, width), jnp.float32)
                base, nxt, side = zero, zero, zero
                before = None
                for r in range(rows):
                    found = pltpu.matmul_pop(accs[j][r])
                    if more:
                        feed(j, r)
                    if before is not None:
                        nxt = jnp.where(before, found[:levs], nxt)
                    if r < rows - 1:
                        here = jnp.broadcast_to(row == r, (levs, width))
                        base = jnp.where(here, found[:levs], base)
                        side = jnp.where(here, found[levs:], side)
                        before = here
                level = piece(src, 1, j).astype(jnp.int32)
                frac = piece(src, 2, j)
                w0 = piece(src, 3, j)
                w1 = piece(src, 4, j)
                column = w0 * base + w1 * nxt + (1.0 - w0 - w1) * side
                share = jnp.where(lev_iota == level, 1.0 - frac, 0.0)
                share = jnp.where(lev_iota == level + 1, frac, share)
                model = jnp.sum(column * share, axis=0, keepdims=True)
                for t in range(min(2, tiles)):
                    model_buf[src, pl.ds(j * 2 + t, 1)] = model[:, t * 128 : (t + 1) * 128]

            @pl.when(k > 0)
            def _():
                remote(
                    model_buf.at[src],
                    model_in.at[me],
                    model_send.at[src],
                    model_recv.at[me],
                    place(src),
                ).start()

        stage(0)
        for r in range(rows):
            for j in range(chunks):
                feed(j, r)

        def interpolate(k, _):
            src = lax.rem(me + count - k - 1, count)
            remote(
                out_buf.at[src], in_buf.at[src], obs_send.at[src], obs_recv.at[src], place(src)
            ).wait_recv()
            stage(k + 1)
            consume(k, True)
            return 0

        lax.fori_loop(0, count - 1, interpolate, 0)
        consume(count - 1, False)

    pl.run_scoped(
        run,
        [[pltpu.ACC(j)((step_rows, width), jnp.float32) for _ in range(rows)] for j in range(chunks)],
    )
    model_in[me] = model_buf[me]

    def finish(k, _):
        dev = lax.rem(me + count - k, count)

        obs_copy(k).wait_send()
        remote(
            model_buf.at[dev],
            model_in.at[dev],
            model_send.at[dev],
            model_recv.at[dev],
            place(dev),
        ).wait()
        return 0

    lax.fori_loop(1, count, finish, 0)

    def depart(g, _):
        lines = pl.ds(pl.multiple_of(g * 8, 8), 8)
        for t in range(tiles):
            part = pl.ds(t * 128, 128)
            model = jnp.concatenate(
                [model_in[g * 8 + i, pl.ds(t, 1)] for i in range(8)], axis=0
            )
            dep_out[0, lines, part] = mask_ref[0, lines, part].astype(jnp.float32) * (
                values_ref[0, lines, part] - model
            )
        return 0

    lax.fori_loop(0, count // 8, depart, 0)
    stores[3].start()
    for store in stores:
        store.wait()


def hand_over(*refs):
    *pairs, sem = refs
    half = len(pairs) // 2
    copies = [
        pltpu.make_async_copy(src, dst, sem.at[k])
        for k, (src, dst) in enumerate(zip(pairs[:half], pairs[half:]))
    ]
    for copy in copies:
        copy.start()
    for copy in copies:
        copy.wait()


def solution(mesh):
    n_px = mesh.shape["px"]
    n_py = mesh.shape["py"]
    count = n_px * n_py

    def on_device(
        theta_field,
        wind_u,
        wind_v,
        hyper_coef,
        damp_coef,
        obs_cells,
        obs_levels,
        obs_bary,
        obs_vfrac,
        obs_values,
        obs_mask,
    ):
        levs, rows, cols = theta_field.shape
        tiles = obs_values.shape[2] // 128
        hbm = pl.BlockSpec(memory_space=pltpu.HBM)
        smem = pl.BlockSpec(memory_space=pltpu.SMEM)
        f32 = jnp.float32
        i32 = jnp.int32
        bary = jnp.transpose(obs_bary, (0, 2, 1, 3))
        field = jax.ShapeDtypeStruct(theta_field.shape, f32)
        results = pl.pallas_call(
            functools.partial(kernel, (n_px, n_py, tiles)),
            out_shape=(field, field, field, jax.ShapeDtypeStruct(obs_values.shape, f32)),
            in_specs=[smem] * 2 + [hbm] * 9,
            out_specs=[hbm] * 4,
            scratch_shapes=[
                pltpu.VMEM(field.shape, f32),
                pltpu.VMEM(field.shape, f32),
                pltpu.VMEM(field.shape, f32),
                pltpu.VMEM(obs_cells.shape, i32),
                pltpu.VMEM(obs_cells.shape, i32),
                pltpu.VMEM(bary.shape, f32),
                pltpu.VMEM(obs_cells.shape, f32),
                pltpu.VMEM(obs_cells.shape, f32),
                pltpu.VMEM(obs_cells.shape, i32),
                pltpu.VMEM(field.shape, f32),
                pltpu.VMEM(field.shape, f32),
                pltpu.VMEM(field.shape, f32),
                pltpu.VMEM(obs_cells.shape, f32),
                pltpu.VMEM((count, FIELDS, tiles, 128), f32),
                pltpu.VMEM((count, FIELDS, tiles, 128), f32),
                pltpu.VMEM((count, tiles, 128), f32),
                pltpu.VMEM((count, tiles, 128), f32),
                pltpu.VMEM((2, 3, levs // 4, 8, cols), f32),
                pltpu.VMEM((2, 3, levs // 4, 8, cols), f32),
                pltpu.VMEM((levs // 8, rows, cols), f32),
                pltpu.VMEM((2, levs // 8, rows, cols), f32),
                pltpu.VMEM((4, levs // 8, 8, cols), f32),
                pltpu.VMEM((rows * 2 * levs, 2 * cols), jnp.bfloat16),
                pltpu.SemaphoreType.DMA((count,)),
                pltpu.SemaphoreType.DMA((count,)),
                pltpu.SemaphoreType.DMA((count,)),
                pltpu.SemaphoreType.DMA((count,)),
                pltpu.SemaphoreType.DMA((8,)),
                pltpu.SemaphoreType.DMA((8,)),
                pltpu.SemaphoreType.DMA((9,)),
                pltpu.SemaphoreType.DMA((4,)),
            ],
            compiler_params=pltpu.CompilerParams(
                collective_id=0, has_side_effects=True, vmem_limit_bytes=40 * 1024 * 1024
            ),
        )(
            hyper_coef,
            damp_coef,
            wind_u,
            wind_v,
            theta_field,
            obs_cells,
            obs_levels,
            bary,
            obs_vfrac,
            obs_values,
            obs_mask,
        )
        u_next, v_next, t_next, dep = pl.pallas_call(
            hand_over,
            out_shape=[jax.ShapeDtypeStruct(x.shape, x.dtype) for x in results],
            in_specs=[hbm] * 4,
            out_specs=[hbm] * 4,
            scratch_shapes=[pltpu.SemaphoreType.DMA((4,))],
        )(*results)
        return (t_next, u_next, v_next, dep)

    cells = P(None, "px", "py")
    obs = P(("px", "py"), None, None)
    return jax.shard_map(
        on_device,
        mesh=mesh,
        in_specs=(cells, cells, cells, P(), P(), obs, obs, P(("px", "py"), None, None, None), obs, obs, obs),
        out_specs=(cells, cells, cells, obs),
        check_vma=False,
    )
```

```python
import functools

import jax
import jax.numpy as jnp
from jax import lax
from jax.experimental import pallas as pl
from jax.experimental.pallas import tpu as pltpu
from jax.sharding import PartitionSpec as P

MESH = pl.DeviceIdType.MESH
FIELDS = 5
CORNERS = ((-1, -1), (-1, 1), (1, -1), (1, 1))


def laplace(x):
    rows, cols = x.shape
    below = pltpu.roll(x, rows - 1, 0)
    above = pltpu.roll(x, 1, 0)
    return (
        below
        + above
        + pltpu.roll(x + above, cols - 1, 1)
        + pltpu.roll(x + below, 1, 1)
        - 6.0 * x
    )


def diff_x(x):
    return (pltpu.roll(x, x.shape[0] - 1, 0) - pltpu.roll(x, 1, 0)) * 0.5


def diff_y(x):
    return (pltpu.roll(x, x.shape[1] - 1, 1) - pltpu.roll(x, 1, 1)) * 0.5


def kernel(
    sizes,
    hyper,
    damp,
    u_hbm,
    v_hbm,
    t_hbm,
    cells_hbm,
    levels_hbm,
    bary_hbm,
    vfrac_hbm,
    values_hbm,
    mask_hbm,
    u_out,
    v_out,
    t_out,
    dep_out,
    u_ref,
    v_ref,
    t_ref,
    cells_ref,
    levels_ref,
    bary_ref,
    vfrac_ref,
    values_ref,
    mask_ref,
    out_buf,
    in_buf,
    model_buf,
    model_in,
    row_buf,
    row_in,
    col_buf,
    col_in,
    corner_in,
    table,
    obs_send,
    obs_recv,
    model_send,
    model_recv,
    halo_send,
    halo_recv,
    load_sem,
):
    n_px, n_py, tiles = sizes
    count = n_px * n_py
    levs, rows, cols = t_ref.shape
    px = lax.axis_index("px")
    py = lax.axis_index("py")
    me = px * n_py + py
    fields = (u_ref, v_ref, t_ref)

    def place(dev):
        return (dev // n_py, dev % n_py)

    loads = [
        pltpu.make_async_copy(src, dst, load_sem.at[k])
        for k, (src, dst) in enumerate(
            (
                (u_hbm, u_ref),
                (v_hbm, v_ref),
                (t_hbm, t_ref),
                (cells_hbm, cells_ref),
                (levels_hbm, levels_ref),
                (vfrac_hbm, vfrac_ref),
                (bary_hbm, bary_ref),
                (values_hbm, values_ref),
                (mask_hbm, mask_ref),
            )
        )
    ]
    for load in loads:
        load.start()

    barrier = pltpu.get_barrier_semaphore()

    def greet(k, _):
        pl.semaphore_signal(
            barrier, inc=1, device_id=place(lax.rem(me + k, count)), device_id_type=MESH
        )
        return 0

    lax.fori_loop(1, count, greet, 0)

    row8 = lax.broadcasted_iota(jnp.int32, (8, cols), 0)
    lane16 = lax.broadcasted_iota(jnp.int32, (rows, cols), 1)
    lane24 = lax.broadcasted_iota(jnp.int32, (rows + 8, cols), 1)

    for load in loads[:3]:
        load.wait()

    def pack_edges(g, _):
        edge = jnp.zeros((rows, cols), jnp.float32)
        for f, ref in enumerate(fields):
            for half in range(2):
                top = jnp.zeros((8, cols), jnp.float32)
                bottom = top
                for i in range(4):
                    at = half * 4 + i
                    x = ref[g * 8 + at]
                    base = 16 * at + 4 * f
                    edge = jnp.where(
                        lane16 // 4 == base // 4, pltpu.roll(x, (base + 2) % cols, 1), edge
                    )
                    here = row8 // 2 == i
                    head = x[:8]
                    tail = x[rows - 8 :]
                    if i:
                        head = pltpu.roll(head, 2 * i, 0)
                    if (2 * i + 2) % 8:
                        tail = pltpu.roll(tail, 2 * i + 2, 0)
                    top = jnp.where(here, head, top)
                    bottom = jnp.where(here, tail, bottom)
                row_buf[0, f, g * 2 + half] = top
                row_buf[1, f, g * 2 + half] = bottom
        col_buf[g] = edge
        return 0

    lax.fori_loop(0, levs // 8, pack_edges, 0)

    for load in loads[3:]:
        load.wait()

    def pack_obs(g, _):
        lines = pl.ds(pl.multiple_of(g * 8, 8), 8)
        for t in range(tiles):
            part = pl.ds(t * 128, 128)
            whole = (
                cells_ref[0, lines, part].astype(jnp.float32),
                levels_ref[0, lines, part].astype(jnp.float32),
                vfrac_ref[0, lines, part],
                bary_ref[0, 0, lines, part],
                bary_ref[0, 1, lines, part],
            )
            for i in range(8):
                for f, x in enumerate(whole):
                    out_buf[g * 8 + i, f, pl.ds(t, 1)] = x[i : i + 1]
        return 0

    lax.fori_loop(0, count // 8, pack_obs, 0)
    in_buf[me] = out_buf[me]

    pl.semaphore_wait(barrier, count - 1)

    def remote(src, dst, send, recv, dev):
        return pltpu.make_async_remote_copy(
            src_ref=src,
            dst_ref=dst,
            send_sem=send,
            recv_sem=recv,
            device_id=dev,
            device_id_type=MESH,
        )

    up = lax.rem(px + n_px - 1, n_px)
    down = lax.rem(px + 1, n_px)
    left = lax.rem(py + n_py - 1, n_py)
    right = lax.rem(py + 1, n_py)
    halo = []

    def edge_copy(src, dst, dev):
        k = len(halo)
        halo.append(remote(src, dst, halo_send.at[k], halo_recv.at[k], dev))

    edge_copy(row_buf.at[0], row_in.at[0], (up, py))
    edge_copy(row_buf.at[1], row_in.at[1], (down, py))
    edge_copy(col_buf, col_in.at[0], (px, left))
    edge_copy(col_buf, col_in.at[1], (px, right))
    for k, (step_x, step_y) in enumerate(CORNERS):
        part = pl.ds(0, 8) if step_x < 0 else pl.ds(rows - 8, 8)
        edge_copy(
            col_buf.at[:, part],
            corner_in.at[k],
            (up if step_x < 0 else down, left if step_y < 0 else right),
        )
    for copy in halo:
        copy.start()

    def obs_copy(k):
        dev = lax.rem(me + k, count)
        return remote(
            out_buf.at[dev], in_buf.at[me], obs_send.at[dev], obs_recv.at[me], place(dev)
        )

    def send_obs(k, _):
        obs_copy(k).start()
        return 0

    lax.fori_loop(1, count, send_obs, 0)
    for copy in halo:
        copy.wait()

    def advance(g, _):
        low = row8 < 4
        from_left = jnp.concatenate(
            [col_in[1, g // 2], jnp.where(low, corner_in[1, g // 2], corner_in[3, g // 2])], axis=0
        )
        from_right = jnp.concatenate(
            [col_in[0, g // 2], jnp.where(low, corner_in[0, g // 2], corner_in[2, g // 2])], axis=0
        )
        sides = jnp.where(lane24 % 4 < 2, from_left, from_right)
        sides = pltpu.roll(sides, 64 * (g % 2), 1)
        for i in range(4):
            lev = g * 4 + i
            whole = []
            for f, ref in enumerate(fields):
                below = row_in[0, f, g]
                above = row_in[1, f, g]
                if i:
                    below = pltpu.roll(below, 8 - 2 * i, 0)
                if (6 - 2 * i) % 8:
                    above = pltpu.roll(above, 6 - 2 * i, 0)
                middle = jnp.concatenate([ref[lev], jnp.where(low, below, above)], axis=0)
                base = 16 * i + 4 * f
                edge = pltpu.roll(sides, (2 * cols - base - 2) % cols, 1)
                whole.append(jnp.concatenate([middle, edge], axis=1))
            u, v, t = whole
            coef = hyper[lev]
            rate = damp[lev]
            div = diff_x(u) + diff_y(v)
            u_in = u[:rows, :cols]
            v_in = v[:rows, :cols]
            t_in = t[:rows, :cols]
            u_out[lev] = (
                u_in
                - coef * laplace(laplace(u))[:rows, :cols]
                + rate * diff_x(div)[:rows, :cols]
            )
            v_out[lev] = (
                v_in
                - coef * laplace(laplace(v))[:rows, :cols]
                + rate * diff_y(div)[:rows, :cols]
            )
            drift = u_in * diff_x(t)[:rows, :cols] + v_in * diff_y(t)[:rows, :cols]
            t_out[lev] = t_in - coef * laplace(laplace(t))[:rows, :cols] - 0.5 * drift
        return 0

    lax.fori_loop(0, levs // 4, advance, 0)

    for r in range(rows):
        table[pl.ds(r * levs, levs)] = t_out[:, r, :]

    lev_iota = lax.broadcasted_iota(jnp.int32, (levs, 128), 0)

    def pick(x, index):
        return jnp.take_along_axis(x, index, axis=1, mode="promise_in_bounds")

    def interpolate(k, _):
        src = lax.rem(me + count - k, count)

        @pl.when(k > 0)
        def _():
            remote(
                out_buf.at[src], in_buf.at[src], obs_send.at[src], obs_recv.at[src], place(src)
            ).wait_recv()

        for t in range(tiles):

            def piece(f):
                return in_buf[src, f, pl.ds(t, 1)]

            cell = piece(0).astype(jnp.int32)
            row = jnp.broadcast_to(cell // cols, (8, 128))
            col = jnp.broadcast_to(cell & (cols - 1), (8, 128))
            col_next = col + 1
            zero = jnp.zeros((8, 128), jnp.float32)
            base, nxt, side = ([zero] * (levs // 8) for _ in range(3))
            before = None
            for r in range(rows):
                here = row == r
                for part in range(levs // 8):
                    line = table[pl.ds(r * levs + part * 8, 8)]
                    found = pick(line, col)
                    if before is not None:
                        nxt[part] = jnp.where(before, found, nxt[part])
                    if r < rows - 1:
                        base[part] = jnp.where(here, found, base[part])
                        side[part] = jnp.where(here, pick(line, col_next), side[part])
                before = here
            base, nxt, side = (jnp.concatenate(x, axis=0) for x in (base, nxt, side))
            level = piece(1).astype(jnp.int32)
            frac = piece(2)
            w0 = piece(3)
            w1 = piece(4)
            column = w0 * base + w1 * nxt + (1.0 - w0 - w1) * side
            share = jnp.where(lev_iota == level, 1.0 - frac, 0.0)
            share = jnp.where(lev_iota == level + 1, frac, share)
            model_buf[src, pl.ds(t, 1)] = jnp.sum(column * share, axis=0, keepdims=True)

        @pl.when(k > 0)
        def _():
            remote(
                model_buf.at[src],
                model_in.at[me],
                model_send.at[src],
                model_recv.at[me],
                place(src),
            ).start()

        return 0

    lax.fori_loop(0, count, interpolate, 0)
    model_in[me] = model_buf[me]

    def finish(k, _):
        dev = lax.rem(me + count - k, count)

        obs_copy(k).wait_send()
        remote(
            model_buf.at[dev],
            model_in.at[dev],
            model_send.at[dev],
            model_recv.at[dev],
            place(dev),
        ).wait()
        return 0

    lax.fori_loop(1, count, finish, 0)

    def depart(g, _):
        lines = pl.ds(pl.multiple_of(g * 8, 8), 8)
        for t in range(tiles):
            part = pl.ds(t * 128, 128)
            model = jnp.concatenate(
                [model_in[g * 8 + i, pl.ds(t, 1)] for i in range(8)], axis=0
            )
            dep_out[0, lines, part] = mask_ref[0, lines, part].astype(jnp.float32) * (
                values_ref[0, lines, part] - model
            )
        return 0

    lax.fori_loop(0, count // 8, depart, 0)


def hand_over(*refs):
    *pairs, sem = refs
    half = len(pairs) // 2
    copies = [
        pltpu.make_async_copy(src, dst, sem.at[k])
        for k, (src, dst) in enumerate(zip(pairs[:half], pairs[half:]))
    ]
    for copy in copies:
        copy.start()
    for copy in copies:
        copy.wait()


def solution(mesh):
    n_px = mesh.shape["px"]
    n_py = mesh.shape["py"]
    count = n_px * n_py

    def on_device(
        theta_field,
        wind_u,
        wind_v,
        hyper_coef,
        damp_coef,
        obs_cells,
        obs_levels,
        obs_bary,
        obs_vfrac,
        obs_values,
        obs_mask,
    ):
        levs, rows, cols = theta_field.shape
        tiles = obs_values.shape[2] // 128
        hbm = pl.BlockSpec(memory_space=pltpu.HBM)
        vmem = pl.BlockSpec(memory_space=pltpu.VMEM)
        smem = pl.BlockSpec(memory_space=pltpu.SMEM)
        f32 = jnp.float32
        i32 = jnp.int32
        bary = jnp.transpose(obs_bary, (0, 2, 1, 3))
        field = jax.ShapeDtypeStruct(theta_field.shape, f32)
        results = pl.pallas_call(
            functools.partial(kernel, (n_px, n_py, tiles)),
            out_shape=(field, field, field, jax.ShapeDtypeStruct(obs_values.shape, f32)),
            in_specs=[smem] * 2 + [hbm] * 9,
            out_specs=[vmem] * 4,
            scratch_shapes=[
                pltpu.VMEM(field.shape, f32),
                pltpu.VMEM(field.shape, f32),
                pltpu.VMEM(field.shape, f32),
                pltpu.VMEM(obs_cells.shape, i32),
                pltpu.VMEM(obs_cells.shape, i32),
                pltpu.VMEM(bary.shape, f32),
                pltpu.VMEM(obs_cells.shape, f32),
                pltpu.VMEM(obs_cells.shape, f32),
                pltpu.VMEM(obs_cells.shape, i32),
                pltpu.VMEM((count, FIELDS, tiles, 128), f32),
                pltpu.VMEM((count, FIELDS, tiles, 128), f32),
                pltpu.VMEM((count, tiles, 128), f32),
                pltpu.VMEM((count, tiles, 128), f32),
                pltpu.VMEM((2, 3, levs // 4, 8, cols), f32),
                pltpu.VMEM((2, 3, levs // 4, 8, cols), f32),
                pltpu.VMEM((levs // 8, rows, cols), f32),
                pltpu.VMEM((2, levs // 8, rows, cols), f32),
                pltpu.VMEM((4, levs // 8, 8, cols), f32),
                pltpu.VMEM((rows * levs, cols), f32),
                pltpu.SemaphoreType.DMA((count,)),
                pltpu.SemaphoreType.DMA((count,)),
                pltpu.SemaphoreType.DMA((count,)),
                pltpu.SemaphoreType.DMA((count,)),
                pltpu.SemaphoreType.DMA((8,)),
                pltpu.SemaphoreType.DMA((8,)),
                pltpu.SemaphoreType.DMA((9,)),
            ],
            compiler_params=pltpu.CompilerParams(collective_id=0, has_side_effects=True),
        )(
            hyper_coef,
            damp_coef,
            wind_u,
            wind_v,
            theta_field,
            obs_cells,
            obs_levels,
            bary,
            obs_vfrac,
            obs_values,
            obs_mask,
        )
        u_next, v_next, t_next, dep = pl.pallas_call(
            hand_over,
            out_shape=[jax.ShapeDtypeStruct(x.shape, x.dtype) for x in results],
            in_specs=[vmem] * 4,
            out_specs=[hbm] * 4,
            scratch_shapes=[pltpu.SemaphoreType.DMA((4,))],
        )(*results)
        return (t_next, u_next, v_next, dep)

    cells = P(None, "px", "py")
    obs = P(("px", "py"), None, None)
    return jax.shard_map(
        on_device,
        mesh=mesh,
        in_specs=(cells, cells, cells, P(), P(), obs, obs, P(("px", "py"), None, None, None), obs, obs, obs),
        out_specs=(cells, cells, cells, obs),
        check_vma=False,
    )
```

```python
import functools

import jax
import jax.numpy as jnp
from jax import lax
from jax.experimental import pallas as pl
from jax.experimental.pallas import tpu as pltpu
from jax.sharding import PartitionSpec as P

MESH = pl.DeviceIdType.MESH
FIELDS = 5
CORNERS = ((-1, -1), (-1, 1), (1, -1), (1, 1))


def laplace(x):
    rows, cols = x.shape
    below = pltpu.roll(x, rows - 1, 0)
    above = pltpu.roll(x, 1, 0)
    return (
        below
        + above
        + pltpu.roll(x + above, cols - 1, 1)
        + pltpu.roll(x + below, 1, 1)
        - 6.0 * x
    )


def diff_x(x):
    return (pltpu.roll(x, x.shape[0] - 1, 0) - pltpu.roll(x, 1, 0)) * 0.5


def diff_y(x):
    return (pltpu.roll(x, x.shape[1] - 1, 1) - pltpu.roll(x, 1, 1)) * 0.5


def kernel(
    sizes,
    hyper,
    damp,
    u_hbm,
    v_hbm,
    t_hbm,
    cells_hbm,
    levels_hbm,
    bary_hbm,
    vfrac_hbm,
    values_hbm,
    mask_hbm,
    u_out,
    v_out,
    t_out,
    dep_out,
    u_ref,
    v_ref,
    t_ref,
    cells_ref,
    levels_ref,
    bary_ref,
    vfrac_ref,
    values_ref,
    mask_ref,
    out_buf,
    in_buf,
    model_buf,
    model_in,
    row_buf,
    row_in,
    col_buf,
    col_in,
    corner_in,
    table,
    obs_send,
    obs_recv,
    model_send,
    model_recv,
    halo_send,
    halo_recv,
    load_sem,
):
    n_px, n_py, tiles = sizes
    count = n_px * n_py
    levs, rows, cols = t_ref.shape
    px = lax.axis_index("px")
    py = lax.axis_index("py")
    me = px * n_py + py
    fields = (u_ref, v_ref, t_ref)

    def place(dev):
        return (dev // n_py, dev % n_py)

    loads = [
        pltpu.make_async_copy(src, dst, load_sem.at[k])
        for k, (src, dst) in enumerate(
            (
                (u_hbm, u_ref),
                (v_hbm, v_ref),
                (t_hbm, t_ref),
                (cells_hbm, cells_ref),
                (levels_hbm, levels_ref),
                (vfrac_hbm, vfrac_ref),
                (bary_hbm, bary_ref),
                (values_hbm, values_ref),
                (mask_hbm, mask_ref),
            )
        )
    ]
    for load in loads:
        load.start()

    barrier = pltpu.get_barrier_semaphore()

    def greet(k, _):
        pl.semaphore_signal(
            barrier, inc=1, device_id=place(lax.rem(me + k, count)), device_id_type=MESH
        )
        return 0

    lax.fori_loop(1, count, greet, 0)

    row8 = lax.broadcasted_iota(jnp.int32, (8, cols), 0)
    lane16 = lax.broadcasted_iota(jnp.int32, (rows, cols), 1)
    lane24 = lax.broadcasted_iota(jnp.int32, (rows + 8, cols), 1)

    for load in loads[:3]:
        load.wait()

    def pack_edges(g, _):
        edge = jnp.zeros((rows, cols), jnp.float32)
        for f, ref in enumerate(fields):
            for half in range(2):
                top = jnp.zeros((8, cols), jnp.float32)
                bottom = top
                for i in range(4):
                    at = half * 4 + i
                    x = ref[g * 8 + at]
                    base = 16 * at + 4 * f
                    edge = jnp.where(
                        lane16 // 4 == base // 4, pltpu.roll(x, (base + 2) % cols, 1), edge
                    )
                    here = row8 // 2 == i
                    head = x[:8]
                    tail = x[rows - 8 :]
                    if i:
                        head = pltpu.roll(head, 2 * i, 0)
                    if (2 * i + 2) % 8:
                        tail = pltpu.roll(tail, 2 * i + 2, 0)
                    top = jnp.where(here, head, top)
                    bottom = jnp.where(here, tail, bottom)
                row_buf[0, f, g * 2 + half] = top
                row_buf[1, f, g * 2 + half] = bottom
        col_buf[g] = edge
        return 0

    lax.fori_loop(0, levs // 8, pack_edges, 0)

    for load in loads[3:]:
        load.wait()

    def pack_obs(g, _):
        lines = pl.ds(pl.multiple_of(g * 8, 8), 8)
        for t in range(tiles):
            part = pl.ds(t * 128, 128)
            whole = (
                cells_ref[0, lines, part].astype(jnp.float32),
                levels_ref[0, lines, part].astype(jnp.float32),
                vfrac_ref[0, lines, part],
                bary_ref[0, 0, lines, part],
                bary_ref[0, 1, lines, part],
            )
            for i in range(8):
                for f, x in enumerate(whole):
                    out_buf[g * 8 + i, f, pl.ds(t, 1)] = x[i : i + 1]
        return 0

    lax.fori_loop(0, count // 8, pack_obs, 0)
    in_buf[me] = out_buf[me]

    pl.semaphore_wait(barrier, count - 1)

    def remote(src, dst, send, recv, dev):
        return pltpu.make_async_remote_copy(
            src_ref=src,
            dst_ref=dst,
            send_sem=send,
            recv_sem=recv,
            device_id=dev,
            device_id_type=MESH,
        )

    up = lax.rem(px + n_px - 1, n_px)
    down = lax.rem(px + 1, n_px)
    left = lax.rem(py + n_py - 1, n_py)
    right = lax.rem(py + 1, n_py)
    halo = []

    def edge_copy(src, dst, dev):
        k = len(halo)
        halo.append(remote(src, dst, halo_send.at[k], halo_recv.at[k], dev))

    edge_copy(row_buf.at[0], row_in.at[0], (up, py))
    edge_copy(row_buf.at[1], row_in.at[1], (down, py))
    edge_copy(col_buf, col_in.at[0], (px, left))
    edge_copy(col_buf, col_in.at[1], (px, right))
    for k, (step_x, step_y) in enumerate(CORNERS):
        part = pl.ds(0, 8) if step_x < 0 else pl.ds(rows - 8, 8)
        edge_copy(
            col_buf.at[:, part],
            corner_in.at[k],
            (up if step_x < 0 else down, left if step_y < 0 else right),
        )
    for copy in halo:
        copy.start()

    def obs_copy(k):
        dev = lax.rem(me + k, count)
        return remote(
            out_buf.at[dev], in_buf.at[me], obs_send.at[dev], obs_recv.at[me], place(dev)
        )

    def send_obs(k, _):
        obs_copy(k).start()
        return 0

    lax.fori_loop(1, count, send_obs, 0)
    for copy in halo:
        copy.wait()

    def advance(g, _):
        low = row8 < 4
        from_left = jnp.concatenate(
            [col_in[1, g // 2], jnp.where(low, corner_in[1, g // 2], corner_in[3, g // 2])], axis=0
        )
        from_right = jnp.concatenate(
            [col_in[0, g // 2], jnp.where(low, corner_in[0, g // 2], corner_in[2, g // 2])], axis=0
        )
        sides = jnp.where(lane24 % 4 < 2, from_left, from_right)
        sides = pltpu.roll(sides, 64 * (g % 2), 1)
        for i in range(4):
            lev = g * 4 + i
            whole = []
            for f, ref in enumerate(fields):
                below = row_in[0, f, g]
                above = row_in[1, f, g]
                if i:
                    below = pltpu.roll(below, 8 - 2 * i, 0)
                if (6 - 2 * i) % 8:
                    above = pltpu.roll(above, 6 - 2 * i, 0)
                middle = jnp.concatenate([ref[lev], jnp.where(low, below, above)], axis=0)
                base = 16 * i + 4 * f
                edge = pltpu.roll(sides, (2 * cols - base - 2) % cols, 1)
                whole.append(jnp.concatenate([middle, edge], axis=1))
            u, v, t = whole
            coef = hyper[lev]
            rate = damp[lev]
            div = diff_x(u) + diff_y(v)
            u_in = u[:rows, :cols]
            v_in = v[:rows, :cols]
            t_in = t[:rows, :cols]
            u_out[lev] = (
                u_in
                - coef * laplace(laplace(u))[:rows, :cols]
                + rate * diff_x(div)[:rows, :cols]
            )
            v_out[lev] = (
                v_in
                - coef * laplace(laplace(v))[:rows, :cols]
                + rate * diff_y(div)[:rows, :cols]
            )
            drift = u_in * diff_x(t)[:rows, :cols] + v_in * diff_y(t)[:rows, :cols]
            t_out[lev] = t_in - coef * laplace(laplace(t))[:rows, :cols] - 0.5 * drift
        return 0

    lax.fori_loop(0, levs // 4, advance, 0)

    for r in range(rows):
        line = t_out[:, r, :]
        for step in range(2):
            if step:
                line = pltpu.roll(line, cols - 1, 1)
            high = line.astype(jnp.bfloat16)
            low = (line - high.astype(jnp.float32)).astype(jnp.bfloat16)
            at = (r * 2 + step) * levs
            table[pl.ds(at, levs), pl.ds(0, cols)] = high
            table[pl.ds(at, levs), pl.ds(cols, cols)] = low

    chunks = max(1, tiles // 2)
    width = 256
    col_iota = lax.broadcasted_iota(jnp.int32, (cols, width), 0)
    lev_iota = lax.broadcasted_iota(jnp.int32, (levs, width), 0)
    pieces = [(r, step) for r in range(rows) for step in range(2) if r < rows - 1 or not step]

    def piece(src, f, j):
        return jnp.concatenate(
            [in_buf[src, f, pl.ds(min(j * 2 + t, tiles - 1), 1)] for t in range(2)], axis=1
        )

    def stage(k):
        src = lax.rem(me + count - k, count)
        for j in range(chunks):
            col = piece(src, 0, j).astype(jnp.int32) & (cols - 1)
            hot = jnp.where(col_iota == col, 1.0, 0.0).astype(jnp.bfloat16)
            pltpu.matmul_push_rhs(jnp.concatenate([hot, hot], axis=0), 0, j)

    def run(accs):
        def feed(j, p):
            r, step = pieces[p]
            pltpu.matmul_acc_lhs(
                accs[j][p],
                table[pl.ds((r * 2 + step) * levs, levs)],
                load_staged_rhs=0 if p == 0 else None,
            )

        def consume(k, more):
            src = lax.rem(me + count - k, count)
            zero = jnp.zeros((levs, width), jnp.float32)
            base, nxt, side = ([zero] * chunks for _ in range(3))
            row = [piece(src, 0, j).astype(jnp.int32) // cols for j in range(chunks)]
            before = [None] * chunks
            here = [None] * chunks
            for p, (r, step) in enumerate(pieces):
                for j in range(chunks):
                    found = pltpu.matmul_pop(accs[j][p])
                    if more:
                        feed(j, p)
                    if step:
                        side[j] = jnp.where(here[j], found, side[j])
                        continue
                    before[j] = here[j]
                    if r:
                        nxt[j] = jnp.where(before[j], found, nxt[j])
                    if r < rows - 1:
                        here[j] = jnp.broadcast_to(row[j] == r, (levs, width))
                        base[j] = jnp.where(here[j], found, base[j])
            for j in range(chunks):
                level = piece(src, 1, j).astype(jnp.int32)
                frac = piece(src, 2, j)
                w0 = piece(src, 3, j)
                w1 = piece(src, 4, j)
                column = w0 * base[j] + w1 * nxt[j] + (1.0 - w0 - w1) * side[j]
                share = jnp.where(lev_iota == level, 1.0 - frac, 0.0)
                share = jnp.where(lev_iota == level + 1, frac, share)
                model = jnp.sum(column * share, axis=0, keepdims=True)
                for t in range(min(2, tiles)):
                    model_buf[src, pl.ds(j * 2 + t, 1)] = model[:, t * 128 : (t + 1) * 128]

            @pl.when(k > 0)
            def _():
                remote(
                    model_buf.at[src],
                    model_in.at[me],
                    model_send.at[src],
                    model_recv.at[me],
                    place(src),
                ).start()

        stage(0)
        for p in range(len(pieces)):
            for j in range(chunks):
                feed(j, p)

        def interpolate(k, _):
            src = lax.rem(me + count - k - 1, count)
            remote(
                out_buf.at[src], in_buf.at[src], obs_send.at[src], obs_recv.at[src], place(src)
            ).wait_recv()
            stage(k + 1)
            consume(k, True)
            return 0

        lax.fori_loop(0, count - 1, interpolate, 0)
        consume(count - 1, False)

    pl.run_scoped(
        run,
        [[pltpu.ACC(j)((levs, width), jnp.float32) for _ in pieces] for j in range(chunks)],
    )
    model_in[me] = model_buf[me]

    def finish(k, _):
        dev = lax.rem(me + count - k, count)

        obs_copy(k).wait_send()
        remote(
            model_buf.at[dev],
            model_in.at[dev],
            model_send.at[dev],
            model_recv.at[dev],
            place(dev),
        ).wait()
        return 0

    lax.fori_loop(1, count, finish, 0)

    def depart(g, _):
        lines = pl.ds(pl.multiple_of(g * 8, 8), 8)
        for t in range(tiles):
            part = pl.ds(t * 128, 128)
            model = jnp.concatenate(
                [model_in[g * 8 + i, pl.ds(t, 1)] for i in range(8)], axis=0
            )
            dep_out[0, lines, part] = mask_ref[0, lines, part].astype(jnp.float32) * (
                values_ref[0, lines, part] - model
            )
        return 0

    lax.fori_loop(0, count // 8, depart, 0)


def hand_over(*refs):
    *pairs, sem = refs
    half = len(pairs) // 2
    copies = [
        pltpu.make_async_copy(src, dst, sem.at[k])
        for k, (src, dst) in enumerate(zip(pairs[:half], pairs[half:]))
    ]
    for copy in copies:
        copy.start()
    for copy in copies:
        copy.wait()


def solution(mesh):
    n_px = mesh.shape["px"]
    n_py = mesh.shape["py"]
    count = n_px * n_py

    def on_device(
        theta_field,
        wind_u,
        wind_v,
        hyper_coef,
        damp_coef,
        obs_cells,
        obs_levels,
        obs_bary,
        obs_vfrac,
        obs_values,
        obs_mask,
    ):
        levs, rows, cols = theta_field.shape
        tiles = obs_values.shape[2] // 128
        hbm = pl.BlockSpec(memory_space=pltpu.HBM)
        vmem = pl.BlockSpec(memory_space=pltpu.VMEM)
        smem = pl.BlockSpec(memory_space=pltpu.SMEM)
        f32 = jnp.float32
        i32 = jnp.int32
        bary = jnp.transpose(obs_bary, (0, 2, 1, 3))
        field = jax.ShapeDtypeStruct(theta_field.shape, f32)
        results = pl.pallas_call(
            functools.partial(kernel, (n_px, n_py, tiles)),
            out_shape=(field, field, field, jax.ShapeDtypeStruct(obs_values.shape, f32)),
            in_specs=[smem] * 2 + [hbm] * 9,
            out_specs=[vmem] * 4,
            scratch_shapes=[
                pltpu.VMEM(field.shape, f32),
                pltpu.VMEM(field.shape, f32),
                pltpu.VMEM(field.shape, f32),
                pltpu.VMEM(obs_cells.shape, i32),
                pltpu.VMEM(obs_cells.shape, i32),
                pltpu.VMEM(bary.shape, f32),
                pltpu.VMEM(obs_cells.shape, f32),
                pltpu.VMEM(obs_cells.shape, f32),
                pltpu.VMEM(obs_cells.shape, i32),
                pltpu.VMEM((count, FIELDS, tiles, 128), f32),
                pltpu.VMEM((count, FIELDS, tiles, 128), f32),
                pltpu.VMEM((count, tiles, 128), f32),
                pltpu.VMEM((count, tiles, 128), f32),
                pltpu.VMEM((2, 3, levs // 4, 8, cols), f32),
                pltpu.VMEM((2, 3, levs // 4, 8, cols), f32),
                pltpu.VMEM((levs // 8, rows, cols), f32),
                pltpu.VMEM((2, levs // 8, rows, cols), f32),
                pltpu.VMEM((4, levs // 8, 8, cols), f32),
                pltpu.VMEM((rows * 2 * levs, 2 * cols), jnp.bfloat16),
                pltpu.SemaphoreType.DMA((count,)),
                pltpu.SemaphoreType.DMA((count,)),
                pltpu.SemaphoreType.DMA((count,)),
                pltpu.SemaphoreType.DMA((count,)),
                pltpu.SemaphoreType.DMA((8,)),
                pltpu.SemaphoreType.DMA((8,)),
                pltpu.SemaphoreType.DMA((9,)),
            ],
            compiler_params=pltpu.CompilerParams(collective_id=0, has_side_effects=True),
        )(
            hyper_coef,
            damp_coef,
            wind_u,
            wind_v,
            theta_field,
            obs_cells,
            obs_levels,
            bary,
            obs_vfrac,
            obs_values,
            obs_mask,
        )
        u_next, v_next, t_next, dep = pl.pallas_call(
            hand_over,
            out_shape=[jax.ShapeDtypeStruct(x.shape, x.dtype) for x in results],
            in_specs=[vmem] * 4,
            out_specs=[hbm] * 4,
            scratch_shapes=[pltpu.SemaphoreType.DMA((4,))],
        )(*results)
        return (t_next, u_next, v_next, dep)

    cells = P(None, "px", "py")
    obs = P(("px", "py"), None, None)
    return jax.shard_map(
        on_device,
        mesh=mesh,
        in_specs=(cells, cells, cells, P(), P(), obs, obs, P(("px", "py"), None, None, None), obs, obs, obs),
        out_specs=(cells, cells, cells, obs),
        check_vma=False,
    )
```

```python
import functools

import jax
import jax.numpy as jnp
from jax import lax
from jax.experimental import pallas as pl
from jax.experimental.pallas import tpu as pltpu
from jax.sharding import PartitionSpec as P

MESH = pl.DeviceIdType.MESH
FIELDS = 5
CORNERS = ((-1, -1), (-1, 1), (1, -1), (1, 1))


def laplace(x):
    rows, cols = x.shape
    below = pltpu.roll(x, rows - 1, 0)
    above = pltpu.roll(x, 1, 0)
    return (
        below
        + above
        + pltpu.roll(x + above, cols - 1, 1)
        + pltpu.roll(x + below, 1, 1)
        - 6.0 * x
    )


def diff_x(x):
    return (pltpu.roll(x, x.shape[0] - 1, 0) - pltpu.roll(x, 1, 0)) * 0.5


def diff_y(x):
    return (pltpu.roll(x, x.shape[1] - 1, 1) - pltpu.roll(x, 1, 1)) * 0.5


def kernel(
    sizes,
    hyper,
    damp,
    u_hbm,
    v_hbm,
    t_hbm,
    cells_hbm,
    levels_hbm,
    bary_hbm,
    vfrac_hbm,
    values_hbm,
    mask_hbm,
    u_out,
    v_out,
    t_out,
    dep_out,
    u_ref,
    v_ref,
    t_ref,
    cells_ref,
    levels_ref,
    bary_ref,
    vfrac_ref,
    values_ref,
    mask_ref,
    out_buf,
    in_buf,
    model_buf,
    model_in,
    row_buf,
    row_in,
    col_buf,
    col_in,
    corner_in,
    table,
    obs_send,
    obs_recv,
    model_send,
    model_recv,
    halo_send,
    halo_recv,
    load_sem,
):
    n_px, n_py, tiles = sizes
    count = n_px * n_py
    levs, rows, cols = t_ref.shape
    px = lax.axis_index("px")
    py = lax.axis_index("py")
    me = px * n_py + py
    fields = (u_ref, v_ref, t_ref)

    def place(dev):
        return (dev // n_py, dev % n_py)

    loads = [
        pltpu.make_async_copy(src, dst, load_sem.at[k])
        for k, (src, dst) in enumerate(
            (
                (u_hbm, u_ref),
                (v_hbm, v_ref),
                (t_hbm, t_ref),
                (cells_hbm, cells_ref),
                (levels_hbm, levels_ref),
                (vfrac_hbm, vfrac_ref),
                (bary_hbm, bary_ref),
                (values_hbm, values_ref),
                (mask_hbm, mask_ref),
            )
        )
    ]
    for load in loads:
        load.start()

    barrier = pltpu.get_barrier_semaphore()

    def greet(k, _):
        pl.semaphore_signal(
            barrier, inc=1, device_id=place(lax.rem(me + k, count)), device_id_type=MESH
        )
        return 0

    lax.fori_loop(1, count, greet, 0)

    row8 = lax.broadcasted_iota(jnp.int32, (8, cols), 0)
    lane16 = lax.broadcasted_iota(jnp.int32, (rows, cols), 1)
    lane24 = lax.broadcasted_iota(jnp.int32, (rows + 8, cols), 1)

    for load in loads[:3]:
        load.wait()

    def pack_edges(g, _):
        edge = jnp.zeros((rows, cols), jnp.float32)
        for f, ref in enumerate(fields):
            for half in range(2):
                top = jnp.zeros((8, cols), jnp.float32)
                bottom = top
                for i in range(4):
                    at = half * 4 + i
                    x = ref[g * 8 + at]
                    base = 16 * at + 4 * f
                    edge = jnp.where(
                        lane16 // 4 == base // 4, pltpu.roll(x, (base + 2) % cols, 1), edge
                    )
                    here = row8 // 2 == i
                    head = x[:8]
                    tail = x[rows - 8 :]
                    if i:
                        head = pltpu.roll(head, 2 * i, 0)
                    if (2 * i + 2) % 8:
                        tail = pltpu.roll(tail, 2 * i + 2, 0)
                    top = jnp.where(here, head, top)
                    bottom = jnp.where(here, tail, bottom)
                row_buf[0, f, g * 2 + half] = top
                row_buf[1, f, g * 2 + half] = bottom
        col_buf[g] = edge
        return 0

    lax.fori_loop(0, levs // 8, pack_edges, 0)

    for load in loads[3:]:
        load.wait()

    def pack_obs(g, _):
        lines = pl.ds(pl.multiple_of(g * 8, 8), 8)
        for t in range(tiles):
            part = pl.ds(t * 128, 128)
            whole = (
                cells_ref[0, lines, part].astype(jnp.float32),
                levels_ref[0, lines, part].astype(jnp.float32),
                vfrac_ref[0, lines, part],
                bary_ref[0, 0, lines, part],
                bary_ref[0, 1, lines, part],
            )
            for i in range(8):
                for f, x in enumerate(whole):
                    out_buf[g * 8 + i, f, pl.ds(t, 1)] = x[i : i + 1]
        return 0

    lax.fori_loop(0, count // 8, pack_obs, 0)
    in_buf[me] = out_buf[me]

    pl.semaphore_wait(barrier, count - 1)

    def remote(src, dst, send, recv, dev):
        return pltpu.make_async_remote_copy(
            src_ref=src,
            dst_ref=dst,
            send_sem=send,
            recv_sem=recv,
            device_id=dev,
            device_id_type=MESH,
        )

    up = lax.rem(px + n_px - 1, n_px)
    down = lax.rem(px + 1, n_px)
    left = lax.rem(py + n_py - 1, n_py)
    right = lax.rem(py + 1, n_py)
    halo = []

    def edge_copy(src, dst, dev):
        k = len(halo)
        halo.append(remote(src, dst, halo_send.at[k], halo_recv.at[k], dev))

    edge_copy(row_buf.at[0], row_in.at[0], (up, py))
    edge_copy(row_buf.at[1], row_in.at[1], (down, py))
    edge_copy(col_buf, col_in.at[0], (px, left))
    edge_copy(col_buf, col_in.at[1], (px, right))
    for k, (step_x, step_y) in enumerate(CORNERS):
        part = pl.ds(0, 8) if step_x < 0 else pl.ds(rows - 8, 8)
        edge_copy(
            col_buf.at[:, part],
            corner_in.at[k],
            (up if step_x < 0 else down, left if step_y < 0 else right),
        )
    for copy in halo:
        copy.start()

    def obs_copy(k):
        dev = lax.rem(me + k, count)
        return remote(
            out_buf.at[dev], in_buf.at[me], obs_send.at[dev], obs_recv.at[me], place(dev)
        )

    def send_obs(k, _):
        obs_copy(k).start()
        return 0

    lax.fori_loop(1, count, send_obs, 0)
    for copy in halo:
        copy.wait()

    def advance(g, _):
        low = row8 < 4
        from_left = jnp.concatenate(
            [col_in[1, g // 2], jnp.where(low, corner_in[1, g // 2], corner_in[3, g // 2])], axis=0
        )
        from_right = jnp.concatenate(
            [col_in[0, g // 2], jnp.where(low, corner_in[0, g // 2], corner_in[2, g // 2])], axis=0
        )
        sides = jnp.where(lane24 % 4 < 2, from_left, from_right)
        sides = pltpu.roll(sides, 64 * (g % 2), 1)
        for i in range(4):
            lev = g * 4 + i
            whole = []
            for f, ref in enumerate(fields):
                below = row_in[0, f, g]
                above = row_in[1, f, g]
                if i:
                    below = pltpu.roll(below, 8 - 2 * i, 0)
                if (6 - 2 * i) % 8:
                    above = pltpu.roll(above, 6 - 2 * i, 0)
                middle = jnp.concatenate([ref[lev], jnp.where(low, below, above)], axis=0)
                base = 16 * i + 4 * f
                edge = pltpu.roll(sides, (2 * cols - base - 2) % cols, 1)
                whole.append(jnp.concatenate([middle, edge], axis=1))
            u, v, t = whole
            coef = hyper[lev]
            rate = damp[lev]
            div = diff_x(u) + diff_y(v)
            u_in = u[:rows, :cols]
            v_in = v[:rows, :cols]
            t_in = t[:rows, :cols]
            u_out[lev] = (
                u_in
                - coef * laplace(laplace(u))[:rows, :cols]
                + rate * diff_x(div)[:rows, :cols]
            )
            v_out[lev] = (
                v_in
                - coef * laplace(laplace(v))[:rows, :cols]
                + rate * diff_y(div)[:rows, :cols]
            )
            drift = u_in * diff_x(t)[:rows, :cols] + v_in * diff_y(t)[:rows, :cols]
            t_out[lev] = t_in - coef * laplace(laplace(t))[:rows, :cols] - 0.5 * drift
        return 0

    lax.fori_loop(0, levs // 4, advance, 0)

    for r in range(rows):
        line = t_out[:, r, :]
        for step in range(2):
            if step:
                line = pltpu.roll(line, cols - 1, 1)
            high = line.astype(jnp.bfloat16)
            low = (line - high.astype(jnp.float32)).astype(jnp.bfloat16)
            at = (r * 2 + step) * levs
            table[pl.ds(at, levs), pl.ds(0, cols)] = high
            table[pl.ds(at, levs), pl.ds(cols, cols)] = low

    chunks = max(1, tiles // 2)
    width = 256
    col_iota = lax.broadcasted_iota(jnp.int32, (cols, width), 0)
    lev_iota = lax.broadcasted_iota(jnp.int32, (levs, width), 0)
    def piece(src, f, j):
        return jnp.concatenate(
            [in_buf[src, f, pl.ds(min(j * 2 + t, tiles - 1), 1)] for t in range(2)], axis=1
        )

    def interpolate(k, _):
        src = lax.rem(me + count - k, count)

        @pl.when(k > 0)
        def _():
            remote(
                out_buf.at[src], in_buf.at[src], obs_send.at[src], obs_recv.at[src], place(src)
            ).wait_recv()

        for j in range(chunks):
            cell = piece(src, 0, j).astype(jnp.int32)
            row = cell // cols
            hot = jnp.where(col_iota == (cell & (cols - 1)), 1.0, 0.0).astype(jnp.bfloat16)
            hot = jnp.concatenate([hot, hot], axis=0)
            found = jnp.dot(table[...], hot, preferred_element_type=jnp.float32)
            zero = jnp.zeros((levs, width), jnp.float32)
            base, nxt, side = zero, zero, zero
            before = None
            for r in range(rows):
                at = r * 2 * levs
                line = found[at : at + levs]
                if before is not None:
                    nxt = jnp.where(before, line, nxt)
                if r < rows - 1:
                    here = jnp.broadcast_to(row == r, (levs, width))
                    base = jnp.where(here, line, base)
                    side = jnp.where(here, found[at + levs : at + 2 * levs], side)
                    before = here
            level = piece(src, 1, j).astype(jnp.int32)
            frac = piece(src, 2, j)
            w0 = piece(src, 3, j)
            w1 = piece(src, 4, j)
            column = w0 * base + w1 * nxt + (1.0 - w0 - w1) * side
            share = jnp.where(lev_iota == level, 1.0 - frac, 0.0)
            share = jnp.where(lev_iota == level + 1, frac, share)
            model = jnp.sum(column * share, axis=0, keepdims=True)
            for t in range(min(2, tiles)):
                model_buf[src, pl.ds(j * 2 + t, 1)] = model[:, t * 128 : (t + 1) * 128]

        @pl.when(k > 0)
        def _():
            remote(
                model_buf.at[src],
                model_in.at[me],
                model_send.at[src],
                model_recv.at[me],
                place(src),
            ).start()

        return 0

    lax.fori_loop(0, count, interpolate, 0)
    model_in[me] = model_buf[me]

    def finish(k, _):
        dev = lax.rem(me + count - k, count)

        obs_copy(k).wait_send()
        remote(
            model_buf.at[dev],
            model_in.at[dev],
            model_send.at[dev],
            model_recv.at[dev],
            place(dev),
        ).wait()
        return 0

    lax.fori_loop(1, count, finish, 0)

    def depart(g, _):
        lines = pl.ds(pl.multiple_of(g * 8, 8), 8)
        for t in range(tiles):
            part = pl.ds(t * 128, 128)
            model = jnp.concatenate(
                [model_in[g * 8 + i, pl.ds(t, 1)] for i in range(8)], axis=0
            )
            dep_out[0, lines, part] = mask_ref[0, lines, part].astype(jnp.float32) * (
                values_ref[0, lines, part] - model
            )
        return 0

    lax.fori_loop(0, count // 8, depart, 0)


def hand_over(*refs):
    *pairs, sem = refs
    half = len(pairs) // 2
    copies = [
        pltpu.make_async_copy(src, dst, sem.at[k])
        for k, (src, dst) in enumerate(zip(pairs[:half], pairs[half:]))
    ]
    for copy in copies:
        copy.start()
    for copy in copies:
        copy.wait()


def solution(mesh):
    n_px = mesh.shape["px"]
    n_py = mesh.shape["py"]
    count = n_px * n_py

    def on_device(
        theta_field,
        wind_u,
        wind_v,
        hyper_coef,
        damp_coef,
        obs_cells,
        obs_levels,
        obs_bary,
        obs_vfrac,
        obs_values,
        obs_mask,
    ):
        levs, rows, cols = theta_field.shape
        tiles = obs_values.shape[2] // 128
        hbm = pl.BlockSpec(memory_space=pltpu.HBM)
        vmem = pl.BlockSpec(memory_space=pltpu.VMEM)
        smem = pl.BlockSpec(memory_space=pltpu.SMEM)
        f32 = jnp.float32
        i32 = jnp.int32
        bary = jnp.transpose(obs_bary, (0, 2, 1, 3))
        field = jax.ShapeDtypeStruct(theta_field.shape, f32)
        results = pl.pallas_call(
            functools.partial(kernel, (n_px, n_py, tiles)),
            out_shape=(field, field, field, jax.ShapeDtypeStruct(obs_values.shape, f32)),
            in_specs=[smem] * 2 + [hbm] * 9,
            out_specs=[vmem] * 4,
            scratch_shapes=[
                pltpu.VMEM(field.shape, f32),
                pltpu.VMEM(field.shape, f32),
                pltpu.VMEM(field.shape, f32),
                pltpu.VMEM(obs_cells.shape, i32),
                pltpu.VMEM(obs_cells.shape, i32),
                pltpu.VMEM(bary.shape, f32),
                pltpu.VMEM(obs_cells.shape, f32),
                pltpu.VMEM(obs_cells.shape, f32),
                pltpu.VMEM(obs_cells.shape, i32),
                pltpu.VMEM((count, FIELDS, tiles, 128), f32),
                pltpu.VMEM((count, FIELDS, tiles, 128), f32),
                pltpu.VMEM((count, tiles, 128), f32),
                pltpu.VMEM((count, tiles, 128), f32),
                pltpu.VMEM((2, 3, levs // 4, 8, cols), f32),
                pltpu.VMEM((2, 3, levs // 4, 8, cols), f32),
                pltpu.VMEM((levs // 8, rows, cols), f32),
                pltpu.VMEM((2, levs // 8, rows, cols), f32),
                pltpu.VMEM((4, levs // 8, 8, cols), f32),
                pltpu.VMEM((rows * 2 * levs, 2 * cols), jnp.bfloat16),
                pltpu.SemaphoreType.DMA((count,)),
                pltpu.SemaphoreType.DMA((count,)),
                pltpu.SemaphoreType.DMA((count,)),
                pltpu.SemaphoreType.DMA((count,)),
                pltpu.SemaphoreType.DMA((8,)),
                pltpu.SemaphoreType.DMA((8,)),
                pltpu.SemaphoreType.DMA((9,)),
            ],
            compiler_params=pltpu.CompilerParams(collective_id=0, has_side_effects=True),
        )(
            hyper_coef,
            damp_coef,
            wind_u,
            wind_v,
            theta_field,
            obs_cells,
            obs_levels,
            bary,
            obs_vfrac,
            obs_values,
            obs_mask,
        )
        u_next, v_next, t_next, dep = pl.pallas_call(
            hand_over,
            out_shape=[jax.ShapeDtypeStruct(x.shape, x.dtype) for x in results],
            in_specs=[vmem] * 4,
            out_specs=[hbm] * 4,
            scratch_shapes=[pltpu.SemaphoreType.DMA((4,))],
        )(*results)
        return (t_next, u_next, v_next, dep)

    cells = P(None, "px", "py")
    obs = P(("px", "py"), None, None)
    return jax.shard_map(
        on_device,
        mesh=mesh,
        in_specs=(cells, cells, cells, P(), P(), obs, obs, P(("px", "py"), None, None, None), obs, obs, obs),
        out_specs=(cells, cells, cells, obs),
        check_vma=False,
    )
```

```python
import functools

import jax
import jax.numpy as jnp
from jax import lax
from jax.experimental import pallas as pl
from jax.experimental.pallas import tpu as pltpu
from jax.sharding import PartitionSpec as P

MESH = pl.DeviceIdType.MESH
FIELDS = 5
CORNERS = ((-1, -1), (-1, 1), (1, -1), (1, 1))


def east(lane, main, side):
    last = main.shape[1] - 1
    return (
        pltpu.roll(jnp.where(lane == 0, side, main), last, 1),
        pltpu.roll(jnp.where(lane == 0, main, side), last, 1),
    )


def west(lane, main, side):
    last = main.shape[1] - 1
    return (
        pltpu.roll(jnp.where(lane == last, side, main), 1, 1),
        pltpu.roll(jnp.where(lane == last, main, side), 1, 1),
    )


def laplace(lane, above, mid, below):
    right = east(lane, mid[0] + above[0], mid[1] + above[1])
    left = west(lane, mid[0] + below[0], mid[1] + below[1])
    return [below[k] + above[k] + right[k] + left[k] - 6.0 * mid[k] for k in range(2)]


def diff_y(lane, mid):
    right = east(lane, *mid)
    left = west(lane, *mid)
    return [(right[k] - left[k]) * 0.5 for k in range(2)]


def kernel(
    sizes,
    hyper,
    damp,
    u_hbm,
    v_hbm,
    t_hbm,
    cells_hbm,
    levels_hbm,
    bary_hbm,
    vfrac_hbm,
    values_hbm,
    mask_hbm,
    u_out,
    v_out,
    t_out,
    dep_out,
    u_ref,
    v_ref,
    t_ref,
    cells_ref,
    levels_ref,
    bary_ref,
    vfrac_ref,
    values_ref,
    mask_ref,
    out_buf,
    in_buf,
    model_buf,
    model_in,
    coefs,
    main,
    side,
    lap_main,
    lap_side,
    col_buf,
    col_in,
    corner_in,
    table,
    obs_send,
    obs_recv,
    model_send,
    model_recv,
    halo_send,
    halo_recv,
    load_sem,
):
    n_px, n_py, tiles = sizes
    count = n_px * n_py
    levs, rows, cols = t_ref.shape
    px = lax.axis_index("px")
    py = lax.axis_index("py")
    me = px * n_py + py
    fields = (u_ref, v_ref, t_ref)

    def place(dev):
        return (dev // n_py, dev % n_py)

    loads = [
        pltpu.make_async_copy(src, dst, load_sem.at[k])
        for k, (src, dst) in enumerate(
            (
                (u_hbm, u_ref),
                (v_hbm, v_ref),
                (t_hbm, t_ref),
                (cells_hbm, cells_ref),
                (levels_hbm, levels_ref),
                (vfrac_hbm, vfrac_ref),
                (bary_hbm, bary_ref),
                (values_hbm, values_ref),
                (mask_hbm, mask_ref),
            )
        )
    ]
    for load in loads:
        load.start()

    barrier = pltpu.get_barrier_semaphore()

    def greet(k, _):
        pl.semaphore_signal(
            barrier, inc=1, device_id=place(lax.rem(me + k, count)), device_id_type=MESH
        )
        return 0

    lax.fori_loop(1, count, greet, 0)

    lane = lax.broadcasted_iota(jnp.int32, (levs, cols), 1)
    for l in range(levs):
        coefs[0, pl.ds(l, 1)] = jnp.full((1, cols), hyper[l], jnp.float32)
        coefs[1, pl.ds(l, 1)] = jnp.full((1, cols), damp[l], jnp.float32)
    for load in loads[:3]:
        load.wait()

    for g in range(rows // 8):
        edge = jnp.zeros((levs, cols), jnp.float32)
        for i in range(8):
            for f, ref in enumerate(fields):
                x = ref[:, g * 8 + i, :]
                main[g * 8 + i + 2, f] = x
                base = 16 * i + 4 * f
                edge = jnp.where(lane // 4 == base // 4, pltpu.roll(x, (base + 2) % cols, 1), edge)
        col_buf[g] = edge

    for load in loads[3:]:
        load.wait()

    def pack_obs(g, _):
        lines = pl.ds(pl.multiple_of(g * 8, 8), 8)
        for t in range(tiles):
            part = pl.ds(t * 128, 128)
            whole = (
                cells_ref[0, lines, part].astype(jnp.float32),
                levels_ref[0, lines, part].astype(jnp.float32),
                vfrac_ref[0, lines, part],
                bary_ref[0, 0, lines, part],
                bary_ref[0, 1, lines, part],
            )
            for i in range(8):
                for f, x in enumerate(whole):
                    out_buf[g * 8 + i, f, pl.ds(t, 1)] = x[i : i + 1]
        return 0

    lax.fori_loop(0, count // 8, pack_obs, 0)
    in_buf[me] = out_buf[me]

    pl.semaphore_wait(barrier, count - 1)

    def remote(src, dst, send, recv, dev):
        return pltpu.make_async_remote_copy(
            src_ref=src,
            dst_ref=dst,
            send_sem=send,
            recv_sem=recv,
            device_id=dev,
            device_id_type=MESH,
        )

    up = lax.rem(px + n_px - 1, n_px)
    down = lax.rem(px + 1, n_px)
    left = lax.rem(py + n_py - 1, n_py)
    right = lax.rem(py + 1, n_py)
    halo = []

    def edge_copy(src, dst, dev):
        k = len(halo)
        halo.append(remote(src, dst, halo_send.at[k], halo_recv.at[k], dev))

    edge_copy(main.at[pl.ds(2, 2)], main.at[pl.ds(rows + 2, 2)], (up, py))
    edge_copy(main.at[pl.ds(rows, 2)], main.at[pl.ds(0, 2)], (down, py))
    edge_copy(col_buf, col_in.at[0], (px, left))
    edge_copy(col_buf, col_in.at[1], (px, right))
    for k, (step_x, step_y) in enumerate(CORNERS):
        edge_copy(
            col_buf.at[0 if step_x < 0 else rows // 8 - 1],
            corner_in.at[k],
            (up if step_x < 0 else down, left if step_y < 0 else right),
        )
    for copy in halo:
        copy.start()

    def obs_copy(k):
        dev = lax.rem(me + k, count)
        return remote(
            out_buf.at[dev], in_buf.at[me], obs_send.at[dev], obs_recv.at[me], place(dev)
        )

    def send_obs(k, _):
        obs_copy(k).start()
        return 0

    lax.fori_loop(1, count, send_obs, 0)
    for copy in halo:
        copy.wait()

    from_left = lane % 4 < 2
    edges = [jnp.where(from_left, corner_in[3], corner_in[2])]
    for g in range(rows // 8):
        edges.append(jnp.where(from_left, col_in[1, g], col_in[0, g]))
    edges.append(jnp.where(from_left, corner_in[1], corner_in[0]))
    for e in range(rows + 4):
        at = (e + 6) % 8
        for f in range(3):
            side[e, f] = pltpu.roll(edges[(e + 6) // 8], (2 * cols - 16 * at - 4 * f - 2) % cols, 1)

    def first(e, _):
        def near(f, step):
            return main[e + step, f], side[e + step, f]

        for f in range(3):
            lap = laplace(lane, near(f, -1), near(f, 0), near(f, 1))
            lap_main[e, f] = lap[0]
            lap_side[e, f] = lap[1]
        below, above = near(0, 1), near(0, -1)
        change = diff_y(lane, near(1, 0))
        lap_main[e, 3] = (below[0] - above[0]) * 0.5 + change[0]
        lap_side[e, 3] = (below[1] - above[1]) * 0.5 + change[1]
        return 0

    lax.fori_loop(1, rows + 3, first, 0)

    for r in range(rows):
        e = r + 2

        def lap_near(f, step):
            return lap_main[e + step, f], lap_side[e + step, f]

        def second(f):
            return laplace(lane, lap_near(f, -1), lap_near(f, 0), lap_near(f, 1))[0]

        coef = coefs[0]
        rate = coefs[1]
        u, v, t = main[e, 0], main[e, 1], main[e, 2]
        grad_x = (lap_main[e + 1, 3] - lap_main[e - 1, 3]) * 0.5
        grad_y = diff_y(lane, lap_near(3, 0))[0]
        theta_x = (main[e + 1, 2] - main[e - 1, 2]) * 0.5
        theta_y = diff_y(lane, (t, side[e, 2]))[0]
        u_out[:, r, :] = u - coef * second(0) + rate * grad_x
        v_out[:, r, :] = v - coef * second(1) + rate * grad_y
        line = t - coef * second(2) - 0.5 * (u * theta_x + v * theta_y)
        t_out[:, r, :] = line
        for step in range(2):
            if step:
                line = pltpu.roll(line, cols - 1, 1)
            high = line.astype(jnp.bfloat16)
            low = (line - high.astype(jnp.float32)).astype(jnp.bfloat16)
            at = (r * 2 + step) * levs
            table[pl.ds(at, levs), pl.ds(0, cols)] = high
            table[pl.ds(at, levs), pl.ds(cols, cols)] = low

    chunks = max(1, tiles // 2)
    width = 256
    col_iota = lax.broadcasted_iota(jnp.int32, (cols, width), 0)
    lev_iota = lax.broadcasted_iota(jnp.int32, (levs, width), 0)
    def piece(src, f, j):
        return jnp.concatenate(
            [in_buf[src, f, pl.ds(min(j * 2 + t, tiles - 1), 1)] for t in range(2)], axis=1
        )

    def interpolate(k, _):
        src = lax.rem(me + count - k, count)

        @pl.when(k > 0)
        def _():
            remote(
                out_buf.at[src], in_buf.at[src], obs_send.at[src], obs_recv.at[src], place(src)
            ).wait_recv()

        for j in range(chunks):
            cell = piece(src, 0, j).astype(jnp.int32)
            row = cell // cols
            hot = jnp.where(col_iota == (cell & (cols - 1)), 1.0, 0.0).astype(jnp.bfloat16)
            hot = jnp.concatenate([hot, hot], axis=0)
            found = jnp.dot(table[...], hot, preferred_element_type=jnp.float32)
            zero = jnp.zeros((levs, width), jnp.float32)
            base, nxt, beside = zero, zero, zero
            before = None
            for r in range(rows):
                at = r * 2 * levs
                line = found[at : at + levs]
                if before is not None:
                    nxt = jnp.where(before, line, nxt)
                if r < rows - 1:
                    here = jnp.broadcast_to(row == r, (levs, width))
                    base = jnp.where(here, line, base)
                    beside = jnp.where(here, found[at + levs : at + 2 * levs], beside)
                    before = here
            level = piece(src, 1, j).astype(jnp.int32)
            frac = piece(src, 2, j)
            w0 = piece(src, 3, j)
            w1 = piece(src, 4, j)
            column = w0 * base + w1 * nxt + (1.0 - w0 - w1) * beside
            share = jnp.where(lev_iota == level, 1.0 - frac, 0.0)
            share = jnp.where(lev_iota == level + 1, frac, share)
            model = jnp.sum(column * share, axis=0, keepdims=True)
            for t in range(min(2, tiles)):
                model_buf[src, pl.ds(j * 2 + t, 1)] = model[:, t * 128 : (t + 1) * 128]

        @pl.when(k > 0)
        def _():
            remote(
                model_buf.at[src],
                model_in.at[me],
                model_send.at[src],
                model_recv.at[me],
                place(src),
            ).start()

        return 0

    lax.fori_loop(0, count, interpolate, 0)
    model_in[me] = model_buf[me]

    def finish(k, _):
        dev = lax.rem(me + count - k, count)

        obs_copy(k).wait_send()
        remote(
            model_buf.at[dev],
            model_in.at[dev],
            model_send.at[dev],
            model_recv.at[dev],
            place(dev),
        ).wait()
        return 0

    lax.fori_loop(1, count, finish, 0)

    def depart(g, _):
        lines = pl.ds(pl.multiple_of(g * 8, 8), 8)
        for t in range(tiles):
            part = pl.ds(t * 128, 128)
            model = jnp.concatenate(
                [model_in[g * 8 + i, pl.ds(t, 1)] for i in range(8)], axis=0
            )
            dep_out[0, lines, part] = mask_ref[0, lines, part].astype(jnp.float32) * (
                values_ref[0, lines, part] - model
            )
        return 0

    lax.fori_loop(0, count // 8, depart, 0)


def hand_over(*refs):
    *pairs, sem = refs
    half = len(pairs) // 2
    copies = [
        pltpu.make_async_copy(src, dst, sem.at[k])
        for k, (src, dst) in enumerate(zip(pairs[:half], pairs[half:]))
    ]
    for copy in copies:
        copy.start()
    for copy in copies:
        copy.wait()


def solution(mesh):
    n_px = mesh.shape["px"]
    n_py = mesh.shape["py"]
    count = n_px * n_py

    def on_device(
        theta_field,
        wind_u,
        wind_v,
        hyper_coef,
        damp_coef,
        obs_cells,
        obs_levels,
        obs_bary,
        obs_vfrac,
        obs_values,
        obs_mask,
    ):
        levs, rows, cols = theta_field.shape
        tiles = obs_values.shape[2] // 128
        hbm = pl.BlockSpec(memory_space=pltpu.HBM)
        vmem = pl.BlockSpec(memory_space=pltpu.VMEM)
        smem = pl.BlockSpec(memory_space=pltpu.SMEM)
        f32 = jnp.float32
        i32 = jnp.int32
        bary = jnp.transpose(obs_bary, (0, 2, 1, 3))
        field = jax.ShapeDtypeStruct(theta_field.shape, f32)
        results = pl.pallas_call(
            functools.partial(kernel, (n_px, n_py, tiles)),
            out_shape=(field, field, field, jax.ShapeDtypeStruct(obs_values.shape, f32)),
            in_specs=[smem] * 2 + [hbm] * 9,
            out_specs=[vmem] * 4,
            scratch_shapes=[
                pltpu.VMEM(field.shape, f32),
                pltpu.VMEM(field.shape, f32),
                pltpu.VMEM(field.shape, f32),
                pltpu.VMEM(obs_cells.shape, i32),
                pltpu.VMEM(obs_cells.shape, i32),
                pltpu.VMEM(bary.shape, f32),
                pltpu.VMEM(obs_cells.shape, f32),
                pltpu.VMEM(obs_cells.shape, f32),
                pltpu.VMEM(obs_cells.shape, i32),
                pltpu.VMEM((count, FIELDS, tiles, 128), f32),
                pltpu.VMEM((count, FIELDS, tiles, 128), f32),
                pltpu.VMEM((count, tiles, 128), f32),
                pltpu.VMEM((count, tiles, 128), f32),
                pltpu.VMEM((2, levs, cols), f32),
                pltpu.VMEM((rows + 4, 3, levs, cols), f32),
                pltpu.VMEM((rows + 4, 3, levs, cols), f32),
                pltpu.VMEM((rows + 4, 4, levs, cols), f32),
                pltpu.VMEM((rows + 4, 4, levs, cols), f32),
                pltpu.VMEM((rows // 8, levs, cols), f32),
                pltpu.VMEM((2, rows // 8, levs, cols), f32),
                pltpu.VMEM((4, levs, cols), f32),
                pltpu.VMEM((rows * 2 * levs, 2 * cols), jnp.bfloat16),
                pltpu.SemaphoreType.DMA((count,)),
                pltpu.SemaphoreType.DMA((count,)),
                pltpu.SemaphoreType.DMA((count,)),
                pltpu.SemaphoreType.DMA((count,)),
                pltpu.SemaphoreType.DMA((8,)),
                pltpu.SemaphoreType.DMA((8,)),
                pltpu.SemaphoreType.DMA((9,)),
            ],
            compiler_params=pltpu.CompilerParams(collective_id=0, has_side_effects=True),
        )(
            hyper_coef,
            damp_coef,
            wind_u,
            wind_v,
            theta_field,
            obs_cells,
            obs_levels,
            bary,
            obs_vfrac,
            obs_values,
            obs_mask,
        )
        u_next, v_next, t_next, dep = pl.pallas_call(
            hand_over,
            out_shape=[jax.ShapeDtypeStruct(x.shape, x.dtype) for x in results],
            in_specs=[vmem] * 4,
            out_specs=[hbm] * 4,
            scratch_shapes=[pltpu.SemaphoreType.DMA((4,))],
        )(*results)
        return (t_next, u_next, v_next, dep)

    cells = P(None, "px", "py")
    obs = P(("px", "py"), None, None)
    return jax.shard_map(
        on_device,
        mesh=mesh,
        in_specs=(cells, cells, cells, P(), P(), obs, obs, P(("px", "py"), None, None, None), obs, obs, obs),
        out_specs=(cells, cells, cells, obs),
        check_vma=False,
    )
```

```python
import functools

import jax
import jax.numpy as jnp
from jax import lax
from jax.experimental import pallas as pl
from jax.experimental.pallas import tpu as pltpu
from jax.sharding import PartitionSpec as P

MESH = pl.DeviceIdType.MESH
FIELDS = 5
CORNERS = ((-1, -1), (-1, 1), (1, -1), (1, 1))


def east(lane, main, side):
    last = main.shape[1] - 1
    return (
        pltpu.roll(jnp.where(lane == 0, side, main), last, 1),
        pltpu.roll(jnp.where(lane == 0, main, side), last, 1),
    )


def west(lane, main, side):
    last = main.shape[1] - 1
    return (
        pltpu.roll(jnp.where(lane == last, side, main), 1, 1),
        pltpu.roll(jnp.where(lane == last, main, side), 1, 1),
    )


def laplace(lane, above, mid, below):
    right = east(lane, mid[0] + above[0], mid[1] + above[1])
    left = west(lane, mid[0] + below[0], mid[1] + below[1])
    return [below[k] + above[k] + right[k] + left[k] - 6.0 * mid[k] for k in range(2)]


def diff_y(lane, mid):
    right = east(lane, *mid)
    left = west(lane, *mid)
    return [(right[k] - left[k]) * 0.5 for k in range(2)]


def kernel(
    sizes,
    hyper,
    damp,
    u_hbm,
    v_hbm,
    t_hbm,
    cells_hbm,
    levels_hbm,
    bary_hbm,
    vfrac_hbm,
    values_hbm,
    mask_hbm,
    u_out,
    v_out,
    t_out,
    dep_out,
    u_ref,
    v_ref,
    t_ref,
    cells_ref,
    levels_ref,
    bary_ref,
    vfrac_ref,
    values_ref,
    mask_ref,
    out_buf,
    in_buf,
    model_buf,
    model_in,
    coefs,
    main,
    side,
    lap_main,
    lap_side,
    col_buf,
    col_in,
    corner_in,
    table,
    obs_send,
    obs_recv,
    model_send,
    model_recv,
    halo_send,
    halo_recv,
    load_sem,
):
    n_px, n_py, tiles = sizes
    count = n_px * n_py
    levs, rows, cols = t_ref.shape
    px = lax.axis_index("px")
    py = lax.axis_index("py")
    me = px * n_py + py
    fields = (u_ref, v_ref, t_ref)

    def place(dev):
        return (dev // n_py, dev % n_py)

    loads = [
        pltpu.make_async_copy(src, dst, load_sem.at[k])
        for k, (src, dst) in enumerate(
            (
                (u_hbm, u_ref),
                (v_hbm, v_ref),
                (t_hbm, t_ref),
                (cells_hbm, cells_ref),
                (levels_hbm, levels_ref),
                (vfrac_hbm, vfrac_ref),
                (bary_hbm, bary_ref),
                (values_hbm, values_ref),
                (mask_hbm, mask_ref),
            )
        )
    ]
    for load in loads:
        load.start()

    barrier = pltpu.get_barrier_semaphore()

    def greet(k, _):
        pl.semaphore_signal(
            barrier, inc=1, device_id=place(lax.rem(me + k, count)), device_id_type=MESH
        )
        return 0

    lax.fori_loop(1, count, greet, 0)

    lane = lax.broadcasted_iota(jnp.int32, (levs, cols), 1)
    for l in range(levs):
        coefs[0, pl.ds(l, 1)] = jnp.full((1, cols), hyper[l], jnp.float32)
        coefs[1, pl.ds(l, 1)] = jnp.full((1, cols), damp[l], jnp.float32)
    for load in loads[:3]:
        load.wait()

    for g in range(rows // 8):
        edge = jnp.zeros((levs, cols), jnp.float32)
        for i in range(8):
            for f, ref in enumerate(fields):
                x = ref[:, g * 8 + i, :]
                main[g * 8 + i + 2, f] = x
                base = 16 * i + 4 * f
                edge = jnp.where(lane // 4 == base // 4, pltpu.roll(x, (base + 2) % cols, 1), edge)
        col_buf[g] = edge

    for load in loads[3:]:
        load.wait()

    def pack_obs(g, _):
        lines = pl.ds(pl.multiple_of(g * 8, 8), 8)
        for t in range(tiles):
            part = pl.ds(t * 128, 128)
            whole = (
                cells_ref[0, lines, part].astype(jnp.float32),
                levels_ref[0, lines, part].astype(jnp.float32),
                vfrac_ref[0, lines, part],
                bary_ref[0, 0, lines, part],
                bary_ref[0, 1, lines, part],
            )
            for i in range(8):
                for f, x in enumerate(whole):
                    out_buf[g * 8 + i, f, pl.ds(t, 1)] = x[i : i + 1]
        return 0

    lax.fori_loop(0, count // 8, pack_obs, 0)
    in_buf[me] = out_buf[me]

    pl.semaphore_wait(barrier, count - 1)

    def remote(src, dst, send, recv, dev):
        return pltpu.make_async_remote_copy(
            src_ref=src,
            dst_ref=dst,
            send_sem=send,
            recv_sem=recv,
            device_id=dev,
            device_id_type=MESH,
        )

    up = lax.rem(px + n_px - 1, n_px)
    down = lax.rem(px + 1, n_px)
    left = lax.rem(py + n_py - 1, n_py)
    right = lax.rem(py + 1, n_py)
    halo = []

    def edge_copy(src, dst, dev):
        k = len(halo)
        halo.append(remote(src, dst, halo_send.at[k], halo_recv.at[k], dev))

    edge_copy(main.at[pl.ds(2, 2)], main.at[pl.ds(rows + 2, 2)], (up, py))
    edge_copy(main.at[pl.ds(rows, 2)], main.at[pl.ds(0, 2)], (down, py))
    edge_copy(col_buf, col_in.at[0], (px, left))
    edge_copy(col_buf, col_in.at[1], (px, right))
    for k, (step_x, step_y) in enumerate(CORNERS):
        edge_copy(
            col_buf.at[0 if step_x < 0 else rows // 8 - 1],
            corner_in.at[k],
            (up if step_x < 0 else down, left if step_y < 0 else right),
        )
    for copy in halo:
        copy.start()

    def obs_copy(k):
        dev = lax.rem(me + k, count)
        return remote(
            out_buf.at[dev], in_buf.at[me], obs_send.at[dev], obs_recv.at[me], place(dev)
        )

    def send_obs(k, _):
        obs_copy(k).start()
        return 0

    lax.fori_loop(1, count, send_obs, 0)
    for copy in halo:
        copy.wait()

    from_left = lane % 4 < 2
    edges = [jnp.where(from_left, corner_in[3], corner_in[2])]
    for g in range(rows // 8):
        edges.append(jnp.where(from_left, col_in[1, g], col_in[0, g]))
    edges.append(jnp.where(from_left, corner_in[1], corner_in[0]))
    for e in range(rows + 4):
        at = (e + 6) % 8
        for f in range(3):
            side[e, f] = pltpu.roll(edges[(e + 6) // 8], (2 * cols - 16 * at - 4 * f - 2) % cols, 1)

    def first(e, _):
        def near(f, step):
            return main[e + step, f], side[e + step, f]

        for f in range(3):
            lap = laplace(lane, near(f, -1), near(f, 0), near(f, 1))
            lap_main[e, f] = lap[0]
            lap_side[e, f] = lap[1]
        below, above = near(0, 1), near(0, -1)
        change = diff_y(lane, near(1, 0))
        lap_main[e, 3] = (below[0] - above[0]) * 0.5 + change[0]
        lap_side[e, 3] = (below[1] - above[1]) * 0.5 + change[1]
        return 0

    lax.fori_loop(1, rows + 3, first, 0)

    for r in range(rows):
        e = r + 2

        def lap_near(f, step):
            return lap_main[e + step, f], lap_side[e + step, f]

        def second(f):
            return laplace(lane, lap_near(f, -1), lap_near(f, 0), lap_near(f, 1))[0]

        coef = coefs[0]
        rate = coefs[1]
        u, v, t = main[e, 0], main[e, 1], main[e, 2]
        grad_x = (lap_main[e + 1, 3] - lap_main[e - 1, 3]) * 0.5
        grad_y = diff_y(lane, lap_near(3, 0))[0]
        theta_x = (main[e + 1, 2] - main[e - 1, 2]) * 0.5
        theta_y = diff_y(lane, (t, side[e, 2]))[0]
        u_out[:, r, :] = u - coef * second(0) + rate * grad_x
        v_out[:, r, :] = v - coef * second(1) + rate * grad_y
        line = t - coef * second(2) - 0.5 * (u * theta_x + v * theta_y)
        t_out[:, r, :] = line
        for step in range(2):
            if step:
                line = pltpu.roll(line, cols - 1, 1)
            high = line.astype(jnp.bfloat16)
            low = (line - high.astype(jnp.float32)).astype(jnp.bfloat16)
            at = (r * 2 + step) * levs
            table[pl.ds(at, levs), pl.ds(0, cols)] = high
            table[pl.ds(at, levs), pl.ds(cols, cols)] = low

    chunks = max(1, tiles // 2)
    width = 256
    col_iota = lax.broadcasted_iota(jnp.int32, (cols, width), 0)
    lev_iota = lax.broadcasted_iota(jnp.int32, (levs, width), 0)
    def piece(src, f, j):
        return jnp.concatenate(
            [in_buf[src, f, pl.ds(min(j * 2 + t, tiles - 1), 1)] for t in range(2)], axis=1
        )

    def interpolate(k, _):
        src = lax.rem(me + count - k, count)

        @pl.when(k > 0)
        def _():
            remote(
                out_buf.at[src], in_buf.at[src], obs_send.at[src], obs_recv.at[src], place(src)
            ).wait_recv()

        cells = [piece(src, 0, j).astype(jnp.int32) for j in range(chunks)]
        hot = jnp.concatenate(
            [
                jnp.where(col_iota == (cell & (cols - 1)), 1.0, 0.0).astype(jnp.bfloat16)
                for cell in cells
            ],
            axis=1,
        )
        hot = jnp.concatenate([hot, hot], axis=0)
        products = jnp.dot(table[...], hot, preferred_element_type=jnp.float32)
        for j in range(chunks):
            row = cells[j] // cols
            found = products[:, j * width : (j + 1) * width]
            zero = jnp.zeros((levs, width), jnp.float32)
            base, nxt, beside = zero, zero, zero
            before = None
            for r in range(rows):
                at = r * 2 * levs
                line = found[at : at + levs]
                if before is not None:
                    nxt = jnp.where(before, line, nxt)
                if r < rows - 1:
                    here = jnp.broadcast_to(row == r, (levs, width))
                    base = jnp.where(here, line, base)
                    beside = jnp.where(here, found[at + levs : at + 2 * levs], beside)
                    before = here
            level = piece(src, 1, j).astype(jnp.int32)
            frac = piece(src, 2, j)
            w0 = piece(src, 3, j)
            w1 = piece(src, 4, j)
            column = w0 * base + w1 * nxt + (1.0 - w0 - w1) * beside
            share = jnp.where(lev_iota == level, 1.0 - frac, 0.0)
            share = jnp.where(lev_iota == level + 1, frac, share)
            model = jnp.sum(column * share, axis=0, keepdims=True)
            for t in range(min(2, tiles)):
                model_buf[src, pl.ds(j * 2 + t, 1)] = model[:, t * 128 : (t + 1) * 128]

        @pl.when(k > 0)
        def _():
            remote(
                model_buf.at[src],
                model_in.at[me],
                model_send.at[src],
                model_recv.at[me],
                place(src),
            ).start()

        return 0

    lax.fori_loop(0, count, interpolate, 0)
    model_in[me] = model_buf[me]

    def finish(k, _):
        dev = lax.rem(me + count - k, count)

        obs_copy(k).wait_send()
        remote(
            model_buf.at[dev],
            model_in.at[dev],
            model_send.at[dev],
            model_recv.at[dev],
            place(dev),
        ).wait()
        return 0

    lax.fori_loop(1, count, finish, 0)

    def depart(g, _):
        lines = pl.ds(pl.multiple_of(g * 8, 8), 8)
        for t in range(tiles):
            part = pl.ds(t * 128, 128)
            model = jnp.concatenate(
                [model_in[g * 8 + i, pl.ds(t, 1)] for i in range(8)], axis=0
            )
            dep_out[0, lines, part] = mask_ref[0, lines, part].astype(jnp.float32) * (
                values_ref[0, lines, part] - model
            )
        return 0

    lax.fori_loop(0, count // 8, depart, 0)


def hand_over(*refs):
    *pairs, sem = refs
    half = len(pairs) // 2
    copies = [
        pltpu.make_async_copy(src, dst, sem.at[k])
        for k, (src, dst) in enumerate(zip(pairs[:half], pairs[half:]))
    ]
    for copy in copies:
        copy.start()
    for copy in copies:
        copy.wait()


def solution(mesh):
    n_px = mesh.shape["px"]
    n_py = mesh.shape["py"]
    count = n_px * n_py

    def on_device(
        theta_field,
        wind_u,
        wind_v,
        hyper_coef,
        damp_coef,
        obs_cells,
        obs_levels,
        obs_bary,
        obs_vfrac,
        obs_values,
        obs_mask,
    ):
        levs, rows, cols = theta_field.shape
        tiles = obs_values.shape[2] // 128
        hbm = pl.BlockSpec(memory_space=pltpu.HBM)
        vmem = pl.BlockSpec(memory_space=pltpu.VMEM)
        smem = pl.BlockSpec(memory_space=pltpu.SMEM)
        f32 = jnp.float32
        i32 = jnp.int32
        bary = jnp.transpose(obs_bary, (0, 2, 1, 3))
        field = jax.ShapeDtypeStruct(theta_field.shape, f32)
        results = pl.pallas_call(
            functools.partial(kernel, (n_px, n_py, tiles)),
            out_shape=(field, field, field, jax.ShapeDtypeStruct(obs_values.shape, f32)),
            in_specs=[smem] * 2 + [hbm] * 9,
            out_specs=[vmem] * 4,
            scratch_shapes=[
                pltpu.VMEM(field.shape, f32),
                pltpu.VMEM(field.shape, f32),
                pltpu.VMEM(field.shape, f32),
                pltpu.VMEM(obs_cells.shape, i32),
                pltpu.VMEM(obs_cells.shape, i32),
                pltpu.VMEM(bary.shape, f32),
                pltpu.VMEM(obs_cells.shape, f32),
                pltpu.VMEM(obs_cells.shape, f32),
                pltpu.VMEM(obs_cells.shape, i32),
                pltpu.VMEM((count, FIELDS, tiles, 128), f32),
                pltpu.VMEM((count, FIELDS, tiles, 128), f32),
                pltpu.VMEM((count, tiles, 128), f32),
                pltpu.VMEM((count, tiles, 128), f32),
                pltpu.VMEM((2, levs, cols), f32),
                pltpu.VMEM((rows + 4, 3, levs, cols), f32),
                pltpu.VMEM((rows + 4, 3, levs, cols), f32),
                pltpu.VMEM((rows + 4, 4, levs, cols), f32),
                pltpu.VMEM((rows + 4, 4, levs, cols), f32),
                pltpu.VMEM((rows // 8, levs, cols), f32),
                pltpu.VMEM((2, rows // 8, levs, cols), f32),
                pltpu.VMEM((4, levs, cols), f32),
                pltpu.VMEM((rows * 2 * levs, 2 * cols), jnp.bfloat16),
                pltpu.SemaphoreType.DMA((count,)),
                pltpu.SemaphoreType.DMA((count,)),
                pltpu.SemaphoreType.DMA((count,)),
                pltpu.SemaphoreType.DMA((count,)),
                pltpu.SemaphoreType.DMA((8,)),
                pltpu.SemaphoreType.DMA((8,)),
                pltpu.SemaphoreType.DMA((9,)),
            ],
            compiler_params=pltpu.CompilerParams(collective_id=0, has_side_effects=True),
        )(
            hyper_coef,
            damp_coef,
            wind_u,
            wind_v,
            theta_field,
            obs_cells,
            obs_levels,
            bary,
            obs_vfrac,
            obs_values,
            obs_mask,
        )
        u_next, v_next, t_next, dep = pl.pallas_call(
            hand_over,
            out_shape=[jax.ShapeDtypeStruct(x.shape, x.dtype) for x in results],
            in_specs=[vmem] * 4,
            out_specs=[hbm] * 4,
            scratch_shapes=[pltpu.SemaphoreType.DMA((4,))],
        )(*results)
        return (t_next, u_next, v_next, dep)

    cells = P(None, "px", "py")
    obs = P(("px", "py"), None, None)
    return jax.shard_map(
        on_device,
        mesh=mesh,
        in_specs=(cells, cells, cells, P(), P(), obs, obs, P(("px", "py"), None, None, None), obs, obs, obs),
        out_specs=(cells, cells, cells, obs),
        check_vma=False,
    )
```
